256 devices in a mesh: dur: 32 (over y, z), inc: 8 (over x, core).
Axes of the slice: x: 4, y: 4, z: 8, core: 2. Of those that a mesh axis runs over, the one named last changes fastest.
Arguments:
- value_next: float32 [32, 128, 512], P('dur', 'inc'), may hold values from 0.5 to 2
- markov: float32 [128, 128], replicated, may hold values from 0 to 1, as said below
- energy_share: float32 [32, 128, 512], P('dur', 'inc'), may hold values from 0.1 to 0.5
- bwd_bracket: int32 [2, 32, 128, 512], P(None, 'dur', 'inc'), may hold values from 0 to 510
- bwd_weight: float32 [2, 32, 128, 512], P(None, 'dur', 'inc'), may hold values from 0 to 1
- fwd_bracket: int32 [2, 32, 128, 512], P(None, 'dur', 'inc'), may hold values from 0 to 510
- fwd_weight: float32 [2, 32, 128, 512], P(None, 'dur', 'inc'), may hold values from 0 to 1
- dur_step: int32 [2, 32, 128, 512], P(None, 'dur', 'inc'), may hold values from -1 to 0
- dur_weight: float32 [2, 32, 128, 512], P(None, 'dur', 'inc'), may hold values from 0 to 1
- mass_start: float32 [32, 128, 512], P('dur', 'inc'), may hold values from 0.5 to 1.5
- tax: float32 [2], replicated, may hold values from 0 to 0.5
Outputs:
- value_start: float32 [32, 128, 512], P('dur', 'inc')
- mass_end: float32 [32, 128, 512], P('dur', 'inc')
- demand: float32 [2], replicated
The draws below stay inside these ranges and needn't reach their ends.
Inputs may be any that keep to these rules, and one draw needn't show every extreme that they name: `markov`: entries are positive, each row sums to about one with 0.6 on the diagonal.
All inputs are finite; a program needn't handle non-finite values.
Results may differ from the reference program's by a relative error of at most 0.0001.
Values sent between devices are 32-bit elements; how exact they have to be, the bound alone decides.
No kernel may reach another device: no remote copies, remote signals or barrier semaphores. Data moves between devices by JAX's collectives and lax.ppermute only.
A program may use at most 64 MiB of HBM per device.

```python
import jax
import jax.numpy as jnp
from jax import lax

A = 512
NI = 128
ND = 32


def draw_markov(key, part):
    spread = jax.random.uniform(key, (NI, NI), jnp.float32, 0.0, 2.0)
    return 0.6 * jnp.eye(NI, dtype=jnp.float32) + 0.4 * spread / NI


def with_ends(entries, stream_key, smallest, high):
    spot = [jax.random.randint(jax.random.fold_in(stream_key, axis), (), 0, length) for axis, length in enumerate(entries.shape)]
    longest = entries.shape.index(max(entries.shape))
    next_to = spot[:longest] + [(spot[longest] + 1) % entries.shape[longest]] + spot[longest + 1:]
    return entries.at[tuple(spot)].set(smallest).at[tuple(next_to)].set(high)


def level_of(stream_key, shape, cuts, smallest, high):
    level = 1.0
    for dim, parts in cuts:
        draws = jax.random.uniform(jax.random.fold_in(jax.random.fold_in(stream_key, 6), dim), (parts,), jnp.float32, smallest / len(cuts), high / len(cuts))
        level = level * jnp.repeat(jnp.exp(draws), shape[dim] // parts).reshape((-1,) + (1,) * (len(shape) - 1 - dim))
    return level


def setup_inputs(seed: int = 0) -> dict:
    arg_keys = jax.random.split(jax.random.key(seed), 12)
    return {
        "value_next": jnp.clip(0.5 + 1.5 * jax.random.uniform(arg_keys[0], (ND, NI, A), jnp.float32) ** level_of(arg_keys[0], (ND, NI, A), ((0, 32), (1, 8)), -0.2, 0.2), 0.5, 2.0),
        "markov": draw_markov(jax.random.fold_in(arg_keys[11], 71), 0),
        "energy_share": jnp.clip(0.1 + 0.4 * jax.random.uniform(arg_keys[2], (ND, NI, A), jnp.float32) ** level_of(arg_keys[2], (ND, NI, A), ((0, 32), (1, 8)), -0.2, 0.2), 0.1, 0.5),
        "bwd_bracket": with_ends(jax.random.randint(arg_keys[3], (2, ND, NI, A), 0, A - 1), jax.random.fold_in(arg_keys[3], 1), 0, (A - 1) - 1).astype(jnp.int32),
        "bwd_weight": jnp.clip(1.0 * jax.random.uniform(arg_keys[4], (2, ND, NI, A), jnp.float32) ** level_of(arg_keys[4], (2, ND, NI, A), ((1, 32), (2, 8)), -0.2, 0.2), 0.0, 1.0),
        "fwd_bracket": with_ends(jax.random.randint(arg_keys[5], (2, ND, NI, A), 0, A - 1), jax.random.fold_in(arg_keys[5], 1), 0, (A - 1) - 1).astype(jnp.int32),
        "fwd_weight": jnp.clip(1.0 * jax.random.uniform(arg_keys[6], (2, ND, NI, A), jnp.float32) ** level_of(arg_keys[6], (2, ND, NI, A), ((1, 32), (2, 8)), -0.2, 0.2), 0.0, 1.0),
        "dur_step": with_ends(jax.random.randint(arg_keys[7], (2, ND, NI, A), -1, 1), jax.random.fold_in(arg_keys[7], 1), -1, 0).astype(jnp.int32),
        "dur_weight": jnp.clip(1.0 * jax.random.uniform(arg_keys[8], (2, ND, NI, A), jnp.float32) ** level_of(arg_keys[8], (2, ND, NI, A), ((1, 32), (2, 8)), -0.2, 0.2), 0.0, 1.0),
        "mass_start": jnp.clip(0.5 + 1.0 * jax.random.uniform(arg_keys[9], (ND, NI, A), jnp.float32) ** level_of(arg_keys[9], (ND, NI, A), ((0, 32), (1, 8)), -0.2, 0.2), 0.5, 1.5),
        "tax": jnp.clip(jax.random.uniform(arg_keys[10], (2,), jnp.float32, 0.0, 0.5), 0.0, 0.5),
    }


discount = 0.985
gross_rate = 1.01
adjust_share = 0.3

def markov_apply(field, matrix):
    return jnp.einsum('ij,dja->dia', matrix, field, precision=lax.Precision.HIGHEST)

def smooth_levels(expect):
    lower_side = jnp.concatenate([expect[:1], expect[:-1]], 0)
    upper_side = jnp.concatenate([expect[1:], expect[-1:]], 0)
    return (1.0 - adjust_share) * expect + adjust_share * 0.5 * (lower_side + upper_side)

def push_assets(density, bracket, weight):
    asset_count = density.shape[2]
    flat_rows = density.shape[0] * density.shape[1]
    row_base = (jnp.arange(flat_rows, dtype=jnp.int32) * asset_count)[:, None]
    position = (bracket.reshape(flat_rows, asset_count) + row_base).reshape(-1)
    moved = jnp.zeros((flat_rows * asset_count,), jnp.float32)
    moved = moved.at[position].add(((1.0 - weight) * density).reshape(-1))
    moved = moved.at[position + 1].add((weight * density).reshape(-1))
    return moved.reshape(density.shape)

def reference(value_next, markov, energy_share, bwd_bracket, bwd_weight, fwd_bracket, fwd_weight, dur_step, dur_weight, mass_start, tax):
    marginal = value_next
    energies = [None, None]
    for quarter in (1, 0):
        expect = discount * markov_apply(marginal, markov)
        mixed = smooth_levels(expect)
        bracket = bwd_bracket[quarter]
        lam_weight = bwd_weight[quarter]
        interp = (1.0 - lam_weight) * jnp.take_along_axis(mixed, bracket, axis=2) + lam_weight * jnp.take_along_axis(mixed, bracket + 1, axis=2)
        energies[quarter] = energy_share * lax.rsqrt(interp) / (1.0 + tax[quarter])
        marginal = gross_rate * interp * (1.0 + tax[quarter] * energy_share)
    density = mass_start
    demand_list = []
    scale = 1.0 / (ND * NI * A)
    level_index = jnp.arange(ND, dtype=jnp.int32)[:, None, None]
    for quarter in (0, 1):
        demand_list.append(jnp.sum(density * energies[quarter]) * scale)
        moved = push_assets(density, fwd_bracket[quarter], fwd_weight[quarter])
        lower_level = jnp.clip(level_index + dur_step[quarter], 0, ND - 2)
        offset = lower_level - level_index
        omega = dur_weight[quarter]
        down_flag = (offset == -1).astype(jnp.float32)
        stay_flag = 1.0 - down_flag
        to_minus = moved * (1.0 - omega) * down_flag
        to_self = moved * ((1.0 - omega) * stay_flag + omega * down_flag)
        to_plus = moved * omega * stay_flag
        zero_level = jnp.zeros_like(moved[:1])
        levels_moved = to_self + jnp.concatenate([zero_level, to_plus[:-1]], 0) + jnp.concatenate([to_minus[1:], zero_level], 0)
        density = markov_apply(levels_moved, markov.T)
    return (marginal, density, jnp.stack(demand_list))
```

```python
import jax
import jax.numpy as jnp
from jax import lax
from jax.experimental import pallas as pl
from jax.experimental.pallas import tpu as pltpu
from jax.sharding import PartitionSpec as P

discount = 0.985
gross_rate = 1.01
adjust_share = 0.3

LANES = 128
F32 = jnp.float32
BF16 = jnp.bfloat16
VMEM = pl.BlockSpec(memory_space=pltpu.VMEM)
SMEM = pl.BlockSpec(memory_space=pltpu.SMEM)


def split_bf16(x):
    high = x.astype(BF16)
    return high, (x - high.astype(F32)).astype(BF16)


def bracket_read(mixed, bracket, weight):
    rows, assets = mixed.shape
    upper = pltpu.roll(mixed, assets - 1, 1)
    chunk_of = bracket >> 7
    lane_of = bracket & (LANES - 1)
    pieces = []
    for out in range(assets // LANES):
        span = slice(out * LANES, (out + 1) * LANES)
        lane, chunk = lane_of[:, span], chunk_of[:, span]
        low = high = None
        for source in range(assets // LANES):
            table = slice(source * LANES, (source + 1) * LANES)
            got_low = jnp.take_along_axis(mixed[:, table], lane, axis=1, mode="promise_in_bounds")
            got_high = jnp.take_along_axis(upper[:, table], lane, axis=1, mode="promise_in_bounds")
            low = got_low if source == 0 else jnp.where(chunk == source, got_low, low)
            high = got_high if source == 0 else jnp.where(chunk == source, got_high, high)
        lam = weight[:, span]
        pieces.append((1.0 - lam) * low + lam * high)
    return jnp.concatenate(pieces, axis=1)


def push_assets(density, bracket, weight, parts_ref, sums_ref):
    rows, assets = density.shape
    chunks = assets // LANES
    chunk_of = bracket >> 7
    lane_of = bracket & (LANES - 1)
    share = weight * density
    stay = density - share
    parts = []
    for value in (stay, share):
        high, low = split_bf16(value)
        parts += [high.astype(F32), low.astype(F32)]
    for k, part in enumerate(parts):
        parts_ref[k] = part
    height = 4 * chunks
    place = lax.broadcasted_iota(jnp.int32, (height, assets), 0)
    lane_iota = lax.broadcasted_iota(jnp.int32, (LANES, assets), 0)
    for r in range(rows):
        picked = jnp.broadcast_to(parts_ref[3, r : r + 1, :], (height, assets))
        for k in (2, 1, 0):
            picked = jnp.where(
                place < (k + 1) * chunks, jnp.broadcast_to(parts_ref[k, r : r + 1, :], (height, assets)), picked
            )
        left = jnp.where((place & (chunks - 1)) == chunk_of[r : r + 1, :], picked, 0.0).astype(BF16)
        right = jnp.where(lane_iota == lane_of[r : r + 1, :], 1.0, 0.0).astype(BF16)
        sums_ref[r * height : (r + 1) * height, :] = lax.dot_general(
            left, right, (((1,), (1,)), ((), ())), preferred_element_type=F32
        )

    def gathered(k, h):
        return sums_ref[pl.ds(k * chunks + h, rows, stride=height), :]

    stayed = jnp.concatenate([gathered(0, h) + gathered(1, h) for h in range(chunks)], axis=1)
    shared = jnp.concatenate([gathered(2, h) + gathered(3, h) for h in range(chunks)], axis=1)
    return stayed + pltpu.roll(shared, 1, 1)


def level_shares(moved, step, omega):
    level = lax.axis_index("dur")
    total = lax.axis_size("dur")
    lower = jnp.clip(level + step, 0, total - 2)
    down = lower - level == -1
    upper_part = moved * omega
    lower_part = moved - upper_part
    to_self = jnp.where(down, upper_part, lower_part)
    to_minus = jnp.where(down, lower_part, 0.0)
    to_plus = jnp.where(down, 0.0, upper_part)
    return to_self, to_plus, to_minus


def weights_kernel(markov_ref, out_ref, flip_ref):
    chip = lax.axis_index("inc") // 2
    wide = out_ref.shape[1] // 2
    flip_ref[...] = markov_ref[...].T
    rows = pl.ds(pl.multiple_of(chip * wide, wide), wide)
    for k, matrix in enumerate((flip_ref[rows, :], discount * markov_ref[rows, :])):
        high, low = split_bf16(matrix)
        out_ref[k, :wide, :] = high
        out_ref[k, wide:, :] = low


def open_kernel(
    value_ref, mass_ref, bracket_ref, weight_ref, step_ref, omega_ref, up_ref, down_ref, self_ref, parts_ref, sums_ref
):
    rows = self_ref.shape[0]
    moved = push_assets(mass_ref[0], bracket_ref[0, 0], weight_ref[0, 0], parts_ref, sums_ref)
    to_self, to_plus, to_minus = level_shares(moved, step_ref[0, 0], omega_ref[0, 0])
    self_ref[...] = to_self
    up_ref[:rows, :] = to_plus
    up_ref[rows:, :] = value_ref[0]
    down_ref[:rows, :] = to_minus
    down_ref[rows:, :] = value_ref[0]


def merge_kernel(self_ref, value_ref, from_low_ref, from_high_ref, out_ref):
    rows = self_ref.shape[0]
    level = lax.axis_index("dur")
    value = value_ref[...].reshape(self_ref.shape)
    low = jnp.where(level == 0, value, from_low_ref[rows:, :])
    high = jnp.where(level == lax.axis_size("dur") - 1, value, from_high_ref[rows:, :])
    out_ref[:rows, :] = self_ref[...] + from_low_ref[:rows, :] + from_high_ref[:rows, :]
    out_ref[rows:, :] = (1.0 - adjust_share) * value + adjust_share * 0.5 * (low + high)


def markov_kernel(own_ref, one_ref, two_ref, three_ref, weights_ref, keep_ref, send_ref, field_ref, total_ref):
    inc = lax.axis_index("inc")
    core = inc % 2
    chip = inc // 2
    chips = lax.axis_size("inc") // 2
    rows = own_ref.shape[0] // 2
    wide = 2 * rows
    for k in range(2):
        field_ref[...] = jnp.zeros_like(field_ref)
        for shift, ref in enumerate((own_ref, one_ref, two_ref, three_ref)):
            source = lax.rem(chip + chips - shift, chips)
            at = pl.ds(pl.multiple_of(source * wide + core * rows, rows), rows)
            field_ref[at, :] = ref[k * rows : (k + 1) * rows, :]
        high, low = split_bf16(field_ref[...])
        both = jnp.dot(weights_ref[k], high, preferred_element_type=F32)
        total_ref[k] = both[:wide] + (
            both[wide:] + jnp.dot(weights_ref[k, :wide, :], low, preferred_element_type=F32)
        )
    for k in range(2):
        part = slice(k * rows, (k + 1) * rows)
        keep_ref[part, :] = total_ref[k, pl.ds(pl.multiple_of(core * rows, rows), rows), :]
        send_ref[part, :] = total_ref[k, pl.ds(pl.multiple_of((1 - core) * rows, rows), rows), :]


def turn_kernel(
    keep_ref, got_ref, bracket_ref, lam_ref, energy_ref, tax_ref, fwd_bracket_ref, fwd_weight_ref, step_ref, omega_ref,
    up_ref, down_ref, self_ref, value_ref, demand_ref, parts_ref, sums_ref,
):
    rows = self_ref.shape[0]
    density = keep_ref[:rows, :] + got_ref[:rows, :]
    mixed = keep_ref[rows:, :] + got_ref[rows:, :]
    interp = bracket_read(mixed, bracket_ref[1, 0], lam_ref[1, 0])
    tax = tax_ref[1]
    share = energy_ref[0]
    demand_ref[0] = jnp.sum(density * (share * lax.rsqrt(interp))) / (1.0 + tax)
    value = gross_rate * interp * (1.0 + tax * share)
    moved = push_assets(density, fwd_bracket_ref[1, 0], fwd_weight_ref[1, 0], parts_ref, sums_ref)
    to_self, to_plus, to_minus = level_shares(moved, step_ref[1, 0], omega_ref[1, 0])
    self_ref[...] = to_self
    value_ref[...] = value
    up_ref[:rows, :] = to_plus
    up_ref[rows:, :] = value
    down_ref[:rows, :] = to_minus
    down_ref[rows:, :] = value


def close_kernel(
    keep_ref, got_ref, bracket_ref, lam_ref, energy_ref, tax_ref, mass_ref, demand_ref, value_ref, out_ref, terms_ref
):
    rows = keep_ref.shape[0] // 2
    out_ref[0] = keep_ref[:rows, :] + got_ref[:rows, :]
    mixed = keep_ref[rows:, :] + got_ref[rows:, :]
    interp = bracket_read(mixed, bracket_ref[0, 0], lam_ref[0, 0])
    tax = tax_ref[0]
    share = energy_ref[0]
    value_ref[0] = gross_rate * interp * (1.0 + tax * share)
    first = jnp.sum(mass_ref[0] * (share * lax.rsqrt(interp))) / (1.0 + tax)
    lane = lax.broadcasted_iota(jnp.int32, terms_ref.shape, 1)
    terms_ref[...] = jnp.where(lane == 0, first, jnp.where(lane == 1, demand_ref[0], 0.0))


def per_device(
    value_next,
    markov,
    energy_share,
    bwd_bracket,
    bwd_weight,
    fwd_bracket,
    fwd_weight,
    dur_step,
    dur_weight,
    mass_start,
    tax,
):
    _, rows, assets = value_next.shape
    states = markov.shape[0]
    levels = lax.axis_size("dur")
    incs = lax.axis_size("inc")
    scale = 1.0 / (levels * states * assets)
    chunks = assets // LANES
    slab = jax.ShapeDtypeStruct((rows, assets), F32)
    pair = jax.ShapeDtypeStruct((2 * rows, assets), F32)
    block = jax.ShapeDtypeStruct((1, rows, assets), F32)
    push_scratch = [pltpu.VMEM((4, rows, assets), F32), pltpu.VMEM((rows * 4 * chunks, LANES), F32)]
    upward = [(i, i + 1) for i in range(levels - 1)]
    downward = [(i + 1, i) for i in range(levels - 1)]

    weights = pl.pallas_call(
        weights_kernel,
        out_shape=jax.ShapeDtypeStruct((2, 4 * rows, states), BF16),
        in_specs=[VMEM],
        out_specs=VMEM,
        scratch_shapes=[pltpu.VMEM((states, states), F32)],
        name="weights",
    )(markov)

    def rounds(up, down, kept, value):
        from_low = lax.ppermute(up, "dur", upward)
        from_high = lax.ppermute(down, "dur", downward)
        mine = pl.pallas_call(merge_kernel, out_shape=pair, in_specs=[VMEM] * 4, out_specs=VMEM, name="merge")(
            kept, value, from_low, from_high
        )
        shifted = [lax.ppermute(mine, "inc", [(i, (i + 2 * k) % incs) for i in range(incs)]) for k in (1, 2, 3)]
        keep, send = pl.pallas_call(
            markov_kernel,
            out_shape=(pair, pair),
            in_specs=[VMEM] * 5,
            out_specs=(VMEM, VMEM),
            scratch_shapes=[pltpu.VMEM((states, assets), F32), pltpu.VMEM((2, 2 * rows, assets), F32)],
            name="markov",
        )(mine, *shifted, weights)
        return keep, lax.ppermute(send, "inc", [(i, i ^ 1) for i in range(incs)])

    up, down, kept = pl.pallas_call(
        open_kernel,
        out_shape=(pair, pair, slab),
        in_specs=[VMEM] * 6,
        out_specs=(VMEM,) * 3,
        scratch_shapes=push_scratch,
        name="open",
    )(value_next, mass_start, fwd_bracket, fwd_weight, dur_step, dur_weight)
    keep, got = rounds(up, down, kept, value_next)
    up, down, kept, value, second = pl.pallas_call(
        turn_kernel,
        out_shape=(pair, pair, slab, slab, jax.ShapeDtypeStruct((1,), F32)),
        in_specs=[VMEM] * 5 + [SMEM] + [VMEM] * 4,
        out_specs=(VMEM,) * 4 + (SMEM,),
        scratch_shapes=push_scratch,
        name="turn",
    )(keep, got, bwd_bracket, bwd_weight, energy_share, tax, fwd_bracket, fwd_weight, dur_step, dur_weight)
    keep, got = rounds(up, down, kept, value)
    value_start, mass_end, terms = pl.pallas_call(
        close_kernel,
        out_shape=(block, block, jax.ShapeDtypeStruct((1, LANES), F32)),
        in_specs=[VMEM] * 5 + [SMEM, VMEM, SMEM],
        out_specs=(VMEM,) * 3,
        name="close",
    )(keep, got, bwd_bracket, bwd_weight, energy_share, tax, mass_start, second)
    everyone = levels * incs
    every_term = lax.all_to_all(jnp.broadcast_to(terms[None], (everyone, 1, LANES)), ("dur", "inc"), 0, 0)
    demand = jnp.sum(every_term[:, 0, :2], axis=0) * scale
    return (value_start, mass_end, demand)


def solution(mesh):
    return jax.shard_map(
        per_device,
        mesh=mesh,
        in_specs=(
            P("dur", "inc", None),
            P(),
            P("dur", "inc", None),
            P(None, "dur", "inc", None),
            P(None, "dur", "inc", None),
            P(None, "dur", "inc", None),
            P(None, "dur", "inc", None),
            P(None, "dur", "inc", None),
            P(None, "dur", "inc", None),
            P("dur", "inc", None),
            P(),
        ),
        out_specs=(P("dur", "inc", None), P("dur", "inc", None), P()),
        check_vma=False,
    )
```

```python
import functools

import jax
import jax.numpy as jnp
from jax import lax
from jax.experimental import pallas as pl
from jax.experimental.pallas import tpu as pltpu
from jax.sharding import PartitionSpec as P

discount = 0.985
gross_rate = 1.01
adjust_share = 0.3

LANES = 128
F32 = jnp.float32
BF16 = jnp.bfloat16
VMEM = pl.BlockSpec(memory_space=pltpu.VMEM)
SMEM = pl.BlockSpec(memory_space=pltpu.SMEM)


def in_vmem(*arrays):
    return tuple(pltpu.with_memory_space_constraint(x, pltpu.VMEM) for x in arrays)


def split_bf16(x):
    high = x.astype(BF16)
    return high, (x - high.astype(F32)).astype(BF16)


def bracket_read(mixed, bracket, weight):
    rows, assets = mixed.shape
    upper = pltpu.roll(mixed, assets - 1, 1)
    chunk_of = bracket >> 7
    lane_of = bracket & (LANES - 1)
    pieces = []
    for out in range(assets // LANES):
        span = slice(out * LANES, (out + 1) * LANES)
        lane, chunk = lane_of[:, span], chunk_of[:, span]
        low = high = None
        for source in range(assets // LANES):
            table = slice(source * LANES, (source + 1) * LANES)
            got_low = jnp.take_along_axis(mixed[:, table], lane, axis=1, mode="promise_in_bounds")
            got_high = jnp.take_along_axis(upper[:, table], lane, axis=1, mode="promise_in_bounds")
            low = got_low if source == 0 else jnp.where(chunk == source, got_low, low)
            high = got_high if source == 0 else jnp.where(chunk == source, got_high, high)
        lam = weight[:, span]
        pieces.append((1.0 - lam) * low + lam * high)
    return jnp.concatenate(pieces, axis=1)


def push_assets(density, bracket, weight, parts_ref, sums_ref):
    rows, assets = density.shape
    chunks = assets // LANES
    chunk_of = bracket >> 7
    lane_of = bracket & (LANES - 1)
    share = weight * density
    stay = density - share
    parts = []
    for value in (stay, share):
        high, low = split_bf16(value)
        parts += [high.astype(F32), low.astype(F32)]
    for k, part in enumerate(parts):
        parts_ref[k] = part
    height = 4 * chunks
    place = lax.broadcasted_iota(jnp.int32, (height, assets), 0)
    lane_iota = lax.broadcasted_iota(jnp.int32, (LANES, assets), 0)
    for r in range(rows):
        picked = jnp.broadcast_to(parts_ref[3, r : r + 1, :], (height, assets))
        for k in (2, 1, 0):
            picked = jnp.where(
                place < (k + 1) * chunks, jnp.broadcast_to(parts_ref[k, r : r + 1, :], (height, assets)), picked
            )
        left = jnp.where((place & (chunks - 1)) == chunk_of[r : r + 1, :], picked, 0.0).astype(BF16)
        right = jnp.where(lane_iota == lane_of[r : r + 1, :], 1.0, 0.0).astype(BF16)
        sums_ref[r * height : (r + 1) * height, :] = lax.dot_general(
            left, right, (((1,), (1,)), ((), ())), preferred_element_type=F32
        )

    def gathered(k, h):
        return sums_ref[pl.ds(k * chunks + h, rows, stride=height), :]

    stayed = jnp.concatenate([gathered(0, h) + gathered(1, h) for h in range(chunks)], axis=1)
    shared = jnp.concatenate([gathered(2, h) + gathered(3, h) for h in range(chunks)], axis=1)
    return stayed + pltpu.roll(shared, 1, 1)


def level_shares(moved, step, omega):
    level = lax.axis_index("dur")
    total = lax.axis_size("dur")
    lower = jnp.clip(level + step, 0, total - 2)
    down = lower - level == -1
    upper_part = moved * omega
    lower_part = moved - upper_part
    to_self = jnp.where(down, upper_part, lower_part)
    to_minus = jnp.where(down, lower_part, 0.0)
    to_plus = jnp.where(down, 0.0, upper_part)
    return to_self, to_plus, to_minus


def weights_kernel(markov_ref, out_ref, flip_ref):
    chip = lax.axis_index("inc") // 2
    wide = out_ref.shape[1] // 2
    flip_ref[...] = markov_ref[...].T
    rows = pl.ds(pl.multiple_of(chip * wide, wide), wide)
    for k, matrix in enumerate((flip_ref[rows, :], discount * markov_ref[rows, :])):
        high, low = split_bf16(matrix)
        out_ref[k, :wide, :] = high
        out_ref[k, wide:, :] = low


def open_kernel(
    value_ref, mass_ref, bracket_ref, weight_ref, step_ref, omega_ref, up_ref, down_ref, self_ref, parts_ref, sums_ref
):
    rows = self_ref.shape[0]
    moved = push_assets(mass_ref[0], bracket_ref[0, 0], weight_ref[0, 0], parts_ref, sums_ref)
    to_self, to_plus, to_minus = level_shares(moved, step_ref[0, 0], omega_ref[0, 0])
    self_ref[...] = to_self
    up_ref[:rows, :] = to_plus
    up_ref[rows:, :] = value_ref[0]
    down_ref[:rows, :] = to_minus
    down_ref[rows:, :] = value_ref[0]


def merge_kernel(self_ref, value_ref, from_low_ref, from_high_ref, out_ref):
    rows = self_ref.shape[0]
    level = lax.axis_index("dur")
    value = value_ref[...].reshape(self_ref.shape)
    low = jnp.where(level == 0, value, from_low_ref[rows:, :])
    high = jnp.where(level == lax.axis_size("dur") - 1, value, from_high_ref[rows:, :])
    out_ref[:rows, :] = self_ref[...] + from_low_ref[:rows, :] + from_high_ref[:rows, :]
    out_ref[rows:, :] = (1.0 - adjust_share) * value + adjust_share * 0.5 * (low + high)


def markov_kernel(own_ref, one_ref, two_ref, three_ref, weights_ref, keep_ref, send_ref, field_ref, total_ref):
    inc = lax.axis_index("inc")
    core = inc % 2
    chip = inc // 2
    chips = lax.axis_size("inc") // 2
    rows = own_ref.shape[0] // 2
    wide = 2 * rows
    for k in range(2):
        field_ref[...] = jnp.zeros_like(field_ref)
        for shift, ref in enumerate((own_ref, one_ref, two_ref, three_ref)):
            source = lax.rem(chip + chips - shift, chips)
            at = pl.ds(pl.multiple_of(source * wide + core * rows, rows), rows)
            field_ref[at, :] = ref[k * rows : (k + 1) * rows, :]
        high, low = split_bf16(field_ref[...])
        both = jnp.dot(weights_ref[k], high, preferred_element_type=F32)
        total_ref[k] = both[:wide] + (
            both[wide:] + jnp.dot(weights_ref[k, :wide, :], low, preferred_element_type=F32)
        )
    for k in range(2):
        part = slice(k * rows, (k + 1) * rows)
        keep_ref[part, :] = total_ref[k, pl.ds(pl.multiple_of(core * rows, rows), rows), :]
        send_ref[part, :] = total_ref[k, pl.ds(pl.multiple_of((1 - core) * rows, rows), rows), :]


def turn_kernel(
    keep_ref, got_ref, bracket_ref, lam_ref, energy_ref, tax_ref, fwd_bracket_ref, fwd_weight_ref, step_ref, omega_ref,
    up_ref, down_ref, self_ref, value_ref, demand_ref, parts_ref, sums_ref,
):
    rows = self_ref.shape[0]
    density = keep_ref[:rows, :] + got_ref[:rows, :]
    mixed = keep_ref[rows:, :] + got_ref[rows:, :]
    interp = bracket_read(mixed, bracket_ref[1, 0], lam_ref[1, 0])
    tax = tax_ref[1]
    share = energy_ref[0]
    demand_ref[...] = jnp.broadcast_to(jnp.sum(density * (share * lax.rsqrt(interp))) / (1.0 + tax), demand_ref.shape)
    value = gross_rate * interp * (1.0 + tax * share)
    moved = push_assets(density, fwd_bracket_ref[1, 0], fwd_weight_ref[1, 0], parts_ref, sums_ref)
    to_self, to_plus, to_minus = level_shares(moved, step_ref[1, 0], omega_ref[1, 0])
    self_ref[...] = to_self
    value_ref[...] = value
    up_ref[:rows, :] = to_plus
    up_ref[rows:, :] = value
    down_ref[:rows, :] = to_minus
    down_ref[rows:, :] = value


def close_kernel(
    scale, keep_ref, got_ref, bracket_ref, lam_ref, energy_ref, tax_ref, mass_ref, demand_ref, value_ref, out_ref, terms_ref
):
    rows = keep_ref.shape[0] // 2
    out_ref[0] = keep_ref[:rows, :] + got_ref[:rows, :]
    mixed = keep_ref[rows:, :] + got_ref[rows:, :]
    interp = bracket_read(mixed, bracket_ref[0, 0], lam_ref[0, 0])
    tax = tax_ref[0]
    share = energy_ref[0]
    value_ref[0] = gross_rate * interp * (1.0 + tax * share)
    first = jnp.sum(mass_ref[0] * (share * lax.rsqrt(interp))) / (1.0 + tax)
    lane = lax.broadcasted_iota(jnp.int32, demand_ref.shape, 1)
    both = scale * jnp.where(lane == 0, first, demand_ref[...])
    terms_ref[...] = jnp.broadcast_to(both[None], terms_ref.shape)


def demand_kernel(terms_ref, out_ref):
    total = jnp.sum(terms_ref[...], axis=0)
    out_ref[0] = total[0, 0]
    out_ref[1] = total[0, 1]


def per_device(
    value_next,
    markov,
    energy_share,
    bwd_bracket,
    bwd_weight,
    fwd_bracket,
    fwd_weight,
    dur_step,
    dur_weight,
    mass_start,
    tax,
):
    _, rows, assets = value_next.shape
    states = markov.shape[0]
    levels = lax.axis_size("dur")
    incs = lax.axis_size("inc")
    scale = 1.0 / (levels * states * assets)
    chunks = assets // LANES
    slab = pltpu.VMEM((rows, assets), F32)
    pair = pltpu.VMEM((2 * rows, assets), F32)
    block = jax.ShapeDtypeStruct((1, rows, assets), F32)
    push_scratch = [pltpu.VMEM((4, rows, assets), F32), pltpu.VMEM((rows * 4 * chunks, LANES), F32)]
    upward = [(i, i + 1) for i in range(levels - 1)]
    downward = [(i + 1, i) for i in range(levels - 1)]
    everyone = levels * incs

    weights = pl.pallas_call(
        weights_kernel,
        out_shape=pltpu.VMEM((2, 4 * rows, states), BF16),
        in_specs=[VMEM],
        out_specs=VMEM,
        scratch_shapes=[pltpu.VMEM((states, states), F32)],
        name="weights",
    )(*in_vmem(markov))

    def rounds(up, down, kept, value):
        from_low = lax.ppermute(up, "dur", upward)
        from_high = lax.ppermute(down, "dur", downward)
        mine = pl.pallas_call(merge_kernel, out_shape=pair, in_specs=[VMEM] * 4, out_specs=VMEM, name="merge")(
            *in_vmem(kept, value, from_low, from_high)
        )
        shifted = [lax.ppermute(mine, "inc", [(i, (i + 2 * k) % incs) for i in range(incs)]) for k in (1, 2, 3)]
        keep, send = pl.pallas_call(
            markov_kernel,
            out_shape=(pair, pair),
            in_specs=[VMEM] * 5,
            out_specs=(VMEM, VMEM),
            scratch_shapes=[pltpu.VMEM((states, assets), F32), pltpu.VMEM((2, 2 * rows, assets), F32)],
            name="markov",
        )(*in_vmem(mine, *shifted, weights))
        return keep, lax.ppermute(send, "inc", [(i, i ^ 1) for i in range(incs)])

    up, down, kept = pl.pallas_call(
        open_kernel,
        out_shape=(pair, pair, slab),
        in_specs=[VMEM] * 6,
        out_specs=(VMEM,) * 3,
        scratch_shapes=push_scratch,
        name="open",
    )(value_next, mass_start, fwd_bracket, fwd_weight, dur_step, dur_weight)
    keep, got = rounds(up, down, kept, value_next)
    up, down, kept, value, second = pl.pallas_call(
        turn_kernel,
        out_shape=(pair, pair, slab, slab, pltpu.VMEM((1, LANES), F32)),
        in_specs=[VMEM] * 5 + [SMEM] + [VMEM] * 4,
        out_specs=(VMEM,) * 5,
        scratch_shapes=push_scratch,
        name="turn",
    )(
        *in_vmem(keep, got, bwd_bracket, bwd_weight, energy_share),
        tax,
        *in_vmem(fwd_bracket, fwd_weight, dur_step, dur_weight),
    )
    keep, got = rounds(up, down, kept, value)
    value_start, mass_end, terms = pl.pallas_call(
        functools.partial(close_kernel, scale),
        out_shape=(block, block, pltpu.VMEM((everyone, 1, LANES), F32)),
        in_specs=[VMEM] * 5 + [SMEM] + [VMEM] * 2,
        out_specs=(VMEM,) * 3,
        name="close",
    )(*in_vmem(keep, got, bwd_bracket, bwd_weight, energy_share), tax, *in_vmem(mass_start, second))
    every_term = lax.all_to_all(terms, ("dur", "inc"), 0, 0)
    demand = pl.pallas_call(
        demand_kernel,
        out_shape=jax.ShapeDtypeStruct((2,), F32),
        in_specs=[VMEM],
        out_specs=SMEM,
        name="demand",
    )(*in_vmem(every_term))
    return (value_start, mass_end, demand)


def solution(mesh):
    return jax.shard_map(
        per_device,
        mesh=mesh,
        in_specs=(
            P("dur", "inc", None),
            P(),
            P("dur", "inc", None),
            P(None, "dur", "inc", None),
            P(None, "dur", "inc", None),
            P(None, "dur", "inc", None),
            P(None, "dur", "inc", None),
            P(None, "dur", "inc", None),
            P(None, "dur", "inc", None),
            P("dur", "inc", None),
            P(),
        ),
        out_specs=(P("dur", "inc", None), P("dur", "inc", None), P()),
        check_vma=False,
    )
```

```python
import functools

import jax
import jax.numpy as jnp
from jax import lax
from jax.experimental import pallas as pl
from jax.experimental.pallas import tpu as pltpu
from jax.sharding import Mesh, PartitionSpec as P

discount = 0.985
gross_rate = 1.01
adjust_share = 0.3

LANES = 128
SHIFTS = (0, 1, 3, 2)
F32 = jnp.float32
BF16 = jnp.bfloat16
VMEM = pl.BlockSpec(memory_space=pltpu.VMEM)
SMEM = pl.BlockSpec(memory_space=pltpu.SMEM)


def in_vmem(*arrays):
    return tuple(pltpu.with_memory_space_constraint(x, pltpu.VMEM) for x in arrays)


def split_bf16(x):
    high = x.astype(BF16)
    return high, (x - high.astype(F32)).astype(BF16)


def bracket_read(mixed, bracket, weight):
    rows, assets = mixed.shape
    upper = pltpu.roll(mixed, assets - 1, 1)
    chunk_of = bracket >> 7
    lane_of = bracket & (LANES - 1)
    pieces = []
    for out in range(assets // LANES):
        span = slice(out * LANES, (out + 1) * LANES)
        lane, chunk = lane_of[:, span], chunk_of[:, span]
        low = high = None
        for source in range(assets // LANES):
            table = slice(source * LANES, (source + 1) * LANES)
            got_low = jnp.take_along_axis(mixed[:, table], lane, axis=1, mode="promise_in_bounds")
            got_high = jnp.take_along_axis(upper[:, table], lane, axis=1, mode="promise_in_bounds")
            low = got_low if source == 0 else jnp.where(chunk == source, got_low, low)
            high = got_high if source == 0 else jnp.where(chunk == source, got_high, high)
        lam = weight[:, span]
        pieces.append((1.0 - lam) * low + lam * high)
    return jnp.concatenate(pieces, axis=1)


def push_assets(density, bracket, weight, parts_ref, sums_ref):
    rows, assets = density.shape
    chunks = assets // LANES
    chunk_of = bracket >> 7
    lane_of = bracket & (LANES - 1)
    share = weight * density
    stay = density - share
    parts = []
    for value in (stay, share):
        high, low = split_bf16(value)
        parts += [high.astype(F32), low.astype(F32)]
    for k, part in enumerate(parts):
        parts_ref[k] = part
    height = 4 * chunks
    place = lax.broadcasted_iota(jnp.int32, (height, assets), 0)
    lane_iota = lax.broadcasted_iota(jnp.int32, (LANES, assets), 0)
    for r in range(rows):
        picked = jnp.broadcast_to(parts_ref[3, r : r + 1, :], (height, assets))
        for k in (2, 1, 0):
            picked = jnp.where(
                place < (k + 1) * chunks, jnp.broadcast_to(parts_ref[k, r : r + 1, :], (height, assets)), picked
            )
        left = jnp.where((place & (chunks - 1)) == chunk_of[r : r + 1, :], picked, 0.0).astype(BF16)
        right = jnp.where(lane_iota == lane_of[r : r + 1, :], 1.0, 0.0).astype(BF16)
        sums_ref[r * height : (r + 1) * height, :] = lax.dot_general(
            left, right, (((1,), (1,)), ((), ())), preferred_element_type=F32
        )

    def gathered(k, h):
        return sums_ref[pl.ds(k * chunks + h, rows, stride=height), :]

    stayed = jnp.concatenate([gathered(0, h) + gathered(1, h) for h in range(chunks)], axis=1)
    shared = jnp.concatenate([gathered(2, h) + gathered(3, h) for h in range(chunks)], axis=1)
    return stayed + pltpu.roll(shared, 1, 1)


def level_shares(moved, step, omega):
    level = lax.axis_index("dur")
    total = lax.axis_size("dur")
    lower = jnp.clip(level + step, 0, total - 2)
    down = lower - level == -1
    upper_part = moved * omega
    lower_part = moved - upper_part
    to_self = jnp.where(down, upper_part, lower_part)
    to_minus = jnp.where(down, lower_part, 0.0)
    to_plus = jnp.where(down, 0.0, upper_part)
    return to_self, to_plus, to_minus


def store_halo(pair_ref, other_ref, to_plus, to_minus, value):
    rows = value.shape[0]
    even = lax.axis_index("dur") % 2 == 0
    pair_ref[:rows, :] = jnp.where(even, to_plus, to_minus)
    other_ref[:rows, :] = jnp.where(even, to_minus, to_plus)
    pair_ref[rows:, :] = value
    other_ref[rows:, :] = value


def weights_kernel(markov_ref, back_ref, ahead_ref, flip_ref):
    chip = lax.axis_index("x")
    states = markov_ref.shape[0]
    wide = ahead_ref.shape[0] // 2
    flip_ref[...] = markov_ref[...].T
    high, low = split_bf16(discount * markov_ref[...])
    back_ref[:states, :] = high
    back_ref[states:, :] = low
    high, low = split_bf16(flip_ref[pl.ds(pl.multiple_of(chip * wide, wide), wide), :])
    ahead_ref[:wide, :] = high
    ahead_ref[wide:, :] = low


def open_kernel(
    scale, value_ref, mass_ref, bracket_ref, weight_ref, step_ref, omega_ref, energy_ref, bwd_bracket_ref, lam_ref,
    tax_ref, pair_ref, other_ref, self_ref, fixed_ref, parts_ref, sums_ref,
):
    rows = self_ref.shape[0]
    moved = push_assets(mass_ref[0], bracket_ref[0, 0], weight_ref[0, 0], parts_ref, sums_ref)
    to_self, to_plus, to_minus = level_shares(moved, step_ref[0, 0], omega_ref[0, 0])
    self_ref[...] = to_self
    store_halo(pair_ref, other_ref, to_plus, to_minus, value_ref[0])
    fixed_ref[:rows, :] = scale * mass_ref[0] * energy_ref[0] / (1.0 + tax_ref[0])
    fixed_ref[rows : 2 * rows, :] = bwd_bracket_ref[0, 0].astype(F32)
    fixed_ref[2 * rows :, :] = lam_ref[0, 0]


def merge_kernel(self_ref, value_ref, other_ref, pair_ref, rider_ref, out_ref):
    rows = self_ref.shape[0]
    level = lax.axis_index("dur")
    value = value_ref[...].reshape(self_ref.shape)
    alone = (level == 0) | (level == lax.axis_size("dur") - 1)
    beside = pair_ref[rows:, :] + jnp.where(alone, value, other_ref[rows:, :])
    incoming = pair_ref[:rows, :] + jnp.where(alone, 0.0, other_ref[:rows, :])
    out_ref[:rows, :] = self_ref[...] + incoming
    out_ref[rows : 2 * rows, :] = (1.0 - adjust_share) * value + adjust_share * 0.5 * beside
    out_ref[2 * rows :, :] = rider_ref[...]


def place_field(refs, part, rows, field_ref):
    chip, core = lax.axis_index("x"), lax.axis_index("core")
    field_ref[...] = jnp.zeros_like(field_ref)
    for shift, ref in zip(SHIFTS, refs):
        at = pl.ds(pl.multiple_of((chip ^ shift) * 2 * rows + core * rows, rows), rows)
        field_ref[at, :] = ref[part * rows : (part + 1) * rows, :]
    return split_bf16(field_ref[...])


def product(factor_high, factor_low, high, low):
    count = factor_high.shape[0]
    both = jnp.dot(jnp.concatenate([factor_high, factor_low], axis=0), high, preferred_element_type=F32)
    return both[:count] + (both[count:] + jnp.dot(factor_high, low, preferred_element_type=F32))


def markov_kernel(
    own_ref, one_ref, two_ref, three_ref, back_ref, ahead_ref, keep_ref, send_ref, field_ref, total_ref
):
    refs = (own_ref, one_ref, two_ref, three_ref)
    chip, core = lax.axis_index("x"), lax.axis_index("core")
    states = back_ref.shape[0] // 2
    wide = ahead_ref.shape[0] // 2
    rows = wide // 2
    mine = pl.ds(pl.multiple_of(core * rows, rows), rows)
    theirs = pl.ds(pl.multiple_of((1 - core) * rows, rows), rows)
    total_ref[:wide, :] = product(ahead_ref[:wide, :], ahead_ref[wide:, :], *place_field(refs, 0, rows, field_ref))
    keep_ref[:rows, :] = total_ref[mine, :]
    send_ref[:rows, :] = total_ref[theirs, :]
    at = pl.multiple_of(chip * wide, wide)
    total_ref[:wide, :] = product(
        back_ref[pl.ds(at, wide), :],
        back_ref[pl.ds(states + at, wide), :],
        *place_field(refs, 1, rows, field_ref),
    )
    keep_ref[rows:, :] = total_ref[mine, :]
    send_ref[rows:, :] = total_ref[theirs, :]


def markov_wide_kernel(
    own_ref, one_ref, two_ref, three_ref, back_ref, ahead_ref, keep_ref, send_ref, demand_ref, field_ref, total_ref,
    terms_ref,
):
    refs = (own_ref, one_ref, two_ref, three_ref)
    chip, core = lax.axis_index("x"), lax.axis_index("core")
    states = back_ref.shape[0] // 2
    wide = ahead_ref.shape[0] // 2
    rows = wide // 2
    mine = pl.ds(pl.multiple_of(core * rows, rows), rows)
    theirs = pl.ds(pl.multiple_of((1 - core) * rows, rows), rows)
    total_ref[:wide, :] = product(ahead_ref[:wide, :], ahead_ref[wide:, :], *place_field(refs, 0, rows, field_ref))
    keep_ref[:rows, :] = total_ref[mine, :]
    send_ref[:rows, :] = total_ref[theirs, :]
    total_ref[...] = product(back_ref[:states, :], back_ref[states:, :], *place_field(refs, 1, rows, field_ref))
    for k in range(len(refs)):
        part = slice((k + 1) * rows, (k + 2) * rows)
        keep_ref[part, :] = total_ref[pl.ds(pl.multiple_of(k * wide + core * rows, rows), rows), :]
        send_ref[part, :] = total_ref[pl.ds(pl.multiple_of(k * wide + (1 - core) * rows, rows), rows), :]
    for shift, ref in zip(SHIFTS, refs):
        terms_ref[chip ^ shift] = ref[2 * rows :, :]
    demand_ref[...] = (terms_ref[0] + terms_ref[1]) + (terms_ref[2] + terms_ref[3])


def turn_kernel(
    scale, keep_ref, got_ref, bracket_ref, lam_ref, energy_ref, tax_ref, fwd_bracket_ref, fwd_weight_ref, step_ref,
    omega_ref, pair_ref, other_ref, self_ref, value_ref, demand_ref, parts_ref, sums_ref,
):
    rows = self_ref.shape[0]
    density = keep_ref[:rows, :] + got_ref[:rows, :]
    mixed = keep_ref[rows:, :] + got_ref[rows:, :]
    interp = bracket_read(mixed, bracket_ref[1, 0], lam_ref[1, 0])
    tax = tax_ref[1]
    share = energy_ref[0]
    spent = density * (share * lax.rsqrt(interp))
    half = demand_ref.shape[0]
    demand_ref[...] = (scale / (1.0 + tax)) * sum(spent[k : k + half] for k in range(0, rows, half))
    value = gross_rate * interp * (1.0 + tax * share)
    moved = push_assets(density, fwd_bracket_ref[1, 0], fwd_weight_ref[1, 0], parts_ref, sums_ref)
    to_self, to_plus, to_minus = level_shares(moved, step_ref[1, 0], omega_ref[1, 0])
    self_ref[...] = to_self
    value_ref[...] = value
    store_halo(pair_ref, other_ref, to_plus, to_minus, value)


def close_kernel(
    keep_ref, got_ref, own_ref, one_ref, two_ref, three_ref, energy_ref, tax_ref, demand_ref,
    value_ref, mass_ref, terms_ref, fixed_ref, interp_ref,
):
    rows = energy_ref.shape[1]
    chip = lax.axis_index("x")
    refs = (own_ref, one_ref, two_ref, three_ref)
    for shift, ref in zip(SHIFTS, refs):
        fixed_ref[chip ^ shift] = ref[2 * rows :, :]
    spent = []
    for k in range(len(refs)):
        part = slice((k + 1) * rows, (k + 2) * rows)
        bracket = fixed_ref[k, rows : 2 * rows, :].astype(jnp.int32)
        interp = bracket_read(keep_ref[part, :] + got_ref[part, :], bracket, fixed_ref[k, 2 * rows :, :])
        interp_ref[k] = interp
        spent.append(fixed_ref[k, :rows, :] * lax.rsqrt(interp))
    first = jnp.sum((spent[0] + spent[1]) + (spent[2] + spent[3]))
    second = jnp.sum(demand_ref[...])
    lane = lax.broadcasted_iota(jnp.int32, terms_ref.shape, 2)
    terms_ref[...] = jnp.where(lane == 0, first, second)
    mass_ref[0] = keep_ref[:rows, :] + got_ref[:rows, :]
    value_ref[0] = gross_rate * interp_ref[chip] * (1.0 + tax_ref[0] * energy_ref[0])


def demand_kernel(terms_ref, out_ref):
    out_ref[...] = jnp.sum(terms_ref[...], axis=0)[0, : out_ref.shape[0]]


def per_device(
    value_next,
    markov,
    energy_share,
    bwd_bracket,
    bwd_weight,
    fwd_bracket,
    fwd_weight,
    dur_step,
    dur_weight,
    mass_start,
    tax,
):
    _, rows, assets = value_next.shape
    states = markov.shape[0]
    levels, chips, cores = (lax.axis_size(axis) for axis in ("dur", "x", "core"))
    scale = 1.0 / (levels * states * assets)
    chunks = assets // LANES
    slab = pltpu.VMEM((rows, assets), F32)
    pair = pltpu.VMEM((2 * rows, assets), F32)
    block = jax.ShapeDtypeStruct((1, rows, assets), F32)
    eight = pltpu.VMEM((8, assets), F32)
    push_scratch = [pltpu.VMEM((4, rows, assets), F32), pltpu.VMEM((rows * 4 * chunks, LANES), F32)]
    pairs = [(i, i ^ 1) for i in range(levels)]
    others = [(i, ((i + 1) ^ 1) - 1) for i in range(1, levels - 1)]

    def over_chips(array):
        return [lax.ppermute(array, "x", [(i, i ^ k) for i in range(chips)]) for k in SHIFTS[1:]]

    def over_cores(array):
        return lax.ppermute(array, "core", [(i, i ^ 1) for i in range(cores)])

    def over_levels(pair_out, other_out):
        other_in = lax.ppermute(other_out, "dur", others)
        return other_in, lax.ppermute(pair_out, "dur", pairs)

    weights = pl.pallas_call(
        weights_kernel,
        out_shape=(pltpu.VMEM((2 * states, states), BF16), pltpu.VMEM((4 * rows, states), BF16)),
        in_specs=[VMEM],
        out_specs=(VMEM, VMEM),
        scratch_shapes=[pltpu.VMEM((states, states), F32)],
        name="weights",
    )(*in_vmem(markov))
    pair_out, other_out, kept, fixed = pl.pallas_call(
        functools.partial(open_kernel, scale),
        out_shape=(pair, pair, slab, pltpu.VMEM((3 * rows, assets), F32)),
        in_specs=[VMEM] * 9 + [SMEM],
        out_specs=(VMEM,) * 4,
        scratch_shapes=push_scratch,
        name="open",
    )(
        value_next, mass_start, fwd_bracket, fwd_weight, dur_step, dur_weight, energy_share, bwd_bracket, bwd_weight, tax
    )
    halo = over_levels(pair_out, other_out)
    mine = pl.pallas_call(
        merge_kernel,
        out_shape=pltpu.VMEM((5 * rows, assets), F32),
        in_specs=[VMEM] * 5,
        out_specs=VMEM,
        name="merge_with_fixed",
    )(*in_vmem(kept, value_next, *halo, fixed))
    every_first = [mine] + over_chips(mine)
    keep, send = pl.pallas_call(
        markov_kernel,
        out_shape=(pair, pair),
        in_specs=[VMEM] * 6,
        out_specs=(VMEM, VMEM),
        scratch_shapes=[pltpu.VMEM((states, assets), F32), pltpu.VMEM((2 * rows, assets), F32)],
        name="markov",
    )(*in_vmem(*every_first, *weights))
    pair_out, other_out, kept, value, second = pl.pallas_call(
        functools.partial(turn_kernel, scale),
        out_shape=(pair, pair, slab, slab, eight),
        in_specs=[VMEM] * 5 + [SMEM] + [VMEM] * 4,
        out_specs=(VMEM,) * 5,
        scratch_shapes=push_scratch,
        name="turn",
    )(
        *in_vmem(keep, over_cores(send), bwd_bracket, bwd_weight, energy_share),
        tax,
        *in_vmem(fwd_bracket, fwd_weight, dur_step, dur_weight),
    )
    halo = over_levels(pair_out, other_out)
    mine = pl.pallas_call(
        merge_kernel,
        out_shape=pltpu.VMEM((2 * rows + 8, assets), F32),
        in_specs=[VMEM] * 5,
        out_specs=VMEM,
        name="merge_with_demand",
    )(*in_vmem(kept, value, *halo, second))
    wide = pltpu.VMEM(((1 + chips) * rows, assets), F32)
    keep, send, second = pl.pallas_call(
        markov_wide_kernel,
        out_shape=(wide, wide, eight),
        in_specs=[VMEM] * 6,
        out_specs=(VMEM,) * 3,
        scratch_shapes=[
            pltpu.VMEM((states, assets), F32),
            pltpu.VMEM((states, assets), F32),
            pltpu.VMEM((chips, 8, assets), F32),
        ],
        name="markov_wide",
    )(*in_vmem(mine, *over_chips(mine), *weights))
    value_start, mass_end, terms = pl.pallas_call(
        close_kernel,
        out_shape=(block, block, pltpu.VMEM((levels * cores, 1, LANES), F32)),
        in_specs=[VMEM] * 7 + [SMEM, VMEM],
        out_specs=(VMEM,) * 3,
        scratch_shapes=[pltpu.VMEM((chips, 3 * rows, assets), F32), pltpu.VMEM((chips, rows, assets), F32)],
        name="close",
    )(*in_vmem(keep, over_cores(send), *every_first, energy_share), tax, *in_vmem(second))
    every_term = lax.all_to_all(terms, ("dur", "core"), 0, 0)
    demand = pl.pallas_call(
        demand_kernel,
        out_shape=jax.ShapeDtypeStruct((2,), F32),
        in_specs=[VMEM],
        out_specs=VMEM,
        name="demand",
    )(*in_vmem(every_term))
    return (value_start, mass_end, demand)


def solution(mesh):
    levels, incs = mesh.devices.shape
    mesh = Mesh(mesh.devices.reshape(levels, incs // 2, 2), ("dur", "x", "core"))
    inc = ("x", "core")
    return jax.shard_map(
        per_device,
        mesh=mesh,
        in_specs=(
            P("dur", inc, None),
            P(),
            P("dur", inc, None),
            P(None, "dur", inc, None),
            P(None, "dur", inc, None),
            P(None, "dur", inc, None),
            P(None, "dur", inc, None),
            P(None, "dur", inc, None),
            P(None, "dur", inc, None),
            P("dur", inc, None),
            P(),
        ),
        out_specs=(P("dur", inc, None), P("dur", inc, None), P()),
        check_vma=False,
    )
```

```python
import functools

import jax
import jax.numpy as jnp
from jax import lax
from jax.experimental import pallas as pl
from jax.experimental.pallas import tpu as pltpu
from jax.sharding import Mesh, PartitionSpec as P

discount = 0.985
gross_rate = 1.01
adjust_share = 0.3

LANES = 128
SHIFTS = (0, 1, 3, 2)
F32 = jnp.float32
BF16 = jnp.bfloat16
VMEM = pl.BlockSpec(memory_space=pltpu.VMEM)
SMEM = pl.BlockSpec(memory_space=pltpu.SMEM)


def in_vmem(*arrays):
    return tuple(pltpu.with_memory_space_constraint(x, pltpu.VMEM) for x in arrays)


def split_bf16(x):
    high = x.astype(BF16)
    return high, (x - high.astype(F32)).astype(BF16)


def bracket_read(mixed, bracket, weight):
    rows, assets = mixed.shape
    chunks = assets // LANES
    upper = pltpu.roll(mixed, assets - 1, 1)
    chunk_of = bracket >> (LANES.bit_length() - 1)
    lane_of = bracket & (LANES - 1)

    def chosen(values, chunk, first):
        if len(values) == 1:
            return values[0]
        half = len(values) // 2
        return jnp.where(
            chunk < first + half, chosen(values[:half], chunk, first), chosen(values[half:], chunk, first + half)
        )

    groups = []
    for top in range(0, rows, 8):
        part = slice(top, top + 8)
        pieces = []
        for out in range(chunks):
            span = slice(out * LANES, (out + 1) * LANES)
            lane, chunk, lam = lane_of[part, span], chunk_of[part, span], weight[part, span]
            low, high = (
                chosen(
                    [
                        jnp.take_along_axis(
                            table[part, k * LANES : (k + 1) * LANES], lane, axis=1, mode="promise_in_bounds"
                        )
                        for k in range(chunks)
                    ],
                    chunk,
                    0,
                )
                for table in (mixed, upper)
            )
            pieces.append((1.0 - lam) * low + lam * high)
        groups.append(jnp.concatenate(pieces, axis=1))
    return jnp.concatenate(groups, axis=0)


def push_assets(density, bracket, weight, parts_ref, sums_ref):
    rows, assets = density.shape
    width = LANES // 2
    chunks = assets // width
    chunk_of = bracket >> (width.bit_length() - 1)
    place_of = bracket & (width - 1)
    share = weight * density
    for k, value in enumerate((density - share, share)):
        high, low = split_bf16(value)
        parts_ref[2 * k] = high.astype(F32)
        parts_ref[2 * k + 1] = low.astype(F32)
    height = 4 * chunks
    chunk_iota = lax.broadcasted_iota(jnp.int32, (chunks, assets), 0)
    place_iota = lax.broadcasted_iota(jnp.int32, (width, assets), 0)
    for r in range(rows):
        row = slice(r, r + 1)
        here = chunk_iota == chunk_of[row, :]
        left = jnp.concatenate([jnp.where(here, parts_ref[k, row, :], 0.0) for k in range(4)], axis=0).astype(BF16)
        right = jnp.where(place_iota == place_of[row, :], 1.0, 0.0).astype(BF16)
        sums_ref[r * height : (r + 1) * height, :width] = lax.dot_general(
            left, right, (((1,), (1,)), ((), ())), preferred_element_type=F32
        )
    low_half = lax.broadcasted_iota(jnp.int32, (rows, LANES), 1) < width

    def gathered(k, h):
        high, low = (sums_ref[pl.ds((k + term) * chunks + h, rows, stride=height), :] for term in range(2))
        return high + low

    def assembled(k):
        return jnp.concatenate(
            [
                jnp.where(low_half, gathered(k, h), pltpu.roll(gathered(k, h + 1), width, 1))
                for h in range(0, chunks, 2)
            ],
            axis=1,
        )

    return assembled(0) + pltpu.roll(assembled(2), 1, 1)


def level_shares(moved, step, omega):
    level = lax.axis_index("dur")
    total = lax.axis_size("dur")
    lower = jnp.clip(level + step, 0, total - 2)
    down = lower - level == -1
    upper_part = moved * omega
    lower_part = moved - upper_part
    to_self = jnp.where(down, upper_part, lower_part)
    to_minus = jnp.where(down, lower_part, 0.0)
    to_plus = jnp.where(down, 0.0, upper_part)
    return to_self, to_plus, to_minus


def store_halo(pair_ref, other_ref, to_plus, to_minus, value):
    rows = value.shape[0]
    even = lax.axis_index("dur") % 2 == 0
    pair_ref[:rows, :] = jnp.where(even, to_plus, to_minus)
    other_ref[:rows, :] = jnp.where(even, to_minus, to_plus)
    pair_ref[rows:, :] = value
    other_ref[rows:, :] = value


def weights_kernel(markov_ref, back_ref, ahead_ref, flip_ref):
    chip = lax.axis_index("x")
    states = markov_ref.shape[0]
    wide = ahead_ref.shape[0] // 2
    flip_ref[...] = markov_ref[...].T
    high, low = split_bf16(discount * markov_ref[...])
    back_ref[:states, :] = high
    back_ref[states:, :] = low
    high, low = split_bf16(flip_ref[pl.ds(pl.multiple_of(chip * wide, wide), wide), :])
    ahead_ref[:wide, :] = high
    ahead_ref[wide:, :] = low


def open_kernel(
    scale, value_ref, mass_ref, bracket_ref, weight_ref, step_ref, omega_ref, energy_ref, bwd_bracket_ref, lam_ref,
    tax_ref, pair_ref, other_ref, self_ref, fixed_ref, parts_ref, sums_ref,
):
    rows = self_ref.shape[0]
    moved = push_assets(mass_ref[0], bracket_ref[0, 0], weight_ref[0, 0], parts_ref, sums_ref)
    to_self, to_plus, to_minus = level_shares(moved, step_ref[0, 0], omega_ref[0, 0])
    self_ref[...] = to_self
    store_halo(pair_ref, other_ref, to_plus, to_minus, value_ref[0])
    fixed_ref[:rows, :] = scale * mass_ref[0] * energy_ref[0] / (1.0 + tax_ref[0])
    fixed_ref[rows : 2 * rows, :] = bwd_bracket_ref[0, 0].astype(F32)
    fixed_ref[2 * rows :, :] = lam_ref[0, 0]


def merge_kernel(self_ref, value_ref, other_ref, pair_ref, rider_ref, out_ref):
    rows = self_ref.shape[0]
    level = lax.axis_index("dur")
    value = value_ref[...].reshape(self_ref.shape)
    alone = (level == 0) | (level == lax.axis_size("dur") - 1)
    beside = pair_ref[rows:, :] + jnp.where(alone, value, other_ref[rows:, :])
    incoming = pair_ref[:rows, :] + jnp.where(alone, 0.0, other_ref[:rows, :])
    out_ref[:rows, :] = self_ref[...] + incoming
    out_ref[rows : 2 * rows, :] = (1.0 - adjust_share) * value + adjust_share * 0.5 * beside
    out_ref[2 * rows :, :] = rider_ref[...]


def place_field(refs, part, rows, field_ref):
    chip, core = lax.axis_index("x"), lax.axis_index("core")
    field_ref[...] = jnp.zeros_like(field_ref)
    for shift, ref in zip(SHIFTS, refs):
        at = pl.ds(pl.multiple_of((chip ^ shift) * 2 * rows + core * rows, rows), rows)
        field_ref[at, :] = ref[part * rows : (part + 1) * rows, :]
    return split_bf16(field_ref[...])


def product(factor_high, factor_low, high, low):
    count = factor_high.shape[0]
    both = jnp.dot(jnp.concatenate([factor_high, factor_low], axis=0), high, preferred_element_type=F32)
    return both[:count] + (both[count:] + jnp.dot(factor_high, low, preferred_element_type=F32))


def markov_kernel(
    own_ref, one_ref, two_ref, three_ref, back_ref, ahead_ref, keep_ref, send_ref, field_ref, total_ref
):
    refs = (own_ref, one_ref, two_ref, three_ref)
    chip, core = lax.axis_index("x"), lax.axis_index("core")
    states = back_ref.shape[0] // 2
    wide = ahead_ref.shape[0] // 2
    rows = wide // 2
    mine = pl.ds(pl.multiple_of(core * rows, rows), rows)
    theirs = pl.ds(pl.multiple_of((1 - core) * rows, rows), rows)
    total_ref[:wide, :] = product(ahead_ref[:wide, :], ahead_ref[wide:, :], *place_field(refs, 0, rows, field_ref))
    keep_ref[:rows, :] = total_ref[mine, :]
    send_ref[:rows, :] = total_ref[theirs, :]
    at = pl.multiple_of(chip * wide, wide)
    total_ref[:wide, :] = product(
        back_ref[pl.ds(at, wide), :],
        back_ref[pl.ds(states + at, wide), :],
        *place_field(refs, 1, rows, field_ref),
    )
    keep_ref[rows:, :] = total_ref[mine, :]
    send_ref[rows:, :] = total_ref[theirs, :]


def markov_wide_kernel(
    own_ref, one_ref, two_ref, three_ref, back_ref, ahead_ref, keep_ref, send_ref, demand_ref, field_ref, total_ref,
    terms_ref,
):
    refs = (own_ref, one_ref, two_ref, three_ref)
    chip, core = lax.axis_index("x"), lax.axis_index("core")
    states = back_ref.shape[0] // 2
    wide = ahead_ref.shape[0] // 2
    rows = wide // 2
    mine = pl.ds(pl.multiple_of(core * rows, rows), rows)
    theirs = pl.ds(pl.multiple_of((1 - core) * rows, rows), rows)
    total_ref[:wide, :] = product(ahead_ref[:wide, :], ahead_ref[wide:, :], *place_field(refs, 0, rows, field_ref))
    keep_ref[:rows, :] = total_ref[mine, :]
    send_ref[:rows, :] = total_ref[theirs, :]
    total_ref[...] = product(back_ref[:states, :], back_ref[states:, :], *place_field(refs, 1, rows, field_ref))
    for k in range(len(refs)):
        part = slice((k + 1) * rows, (k + 2) * rows)
        keep_ref[part, :] = total_ref[pl.ds(pl.multiple_of(k * wide + core * rows, rows), rows), :]
        send_ref[part, :] = total_ref[pl.ds(pl.multiple_of(k * wide + (1 - core) * rows, rows), rows), :]
    for shift, ref in zip(SHIFTS, refs):
        terms_ref[chip ^ shift] = ref[2 * rows :, :]
    demand_ref[...] = (terms_ref[0] + terms_ref[1]) + (terms_ref[2] + terms_ref[3])


def turn_kernel(
    scale, keep_ref, got_ref, bracket_ref, lam_ref, energy_ref, tax_ref, fwd_bracket_ref, fwd_weight_ref, step_ref,
    omega_ref, pair_ref, other_ref, self_ref, value_ref, demand_ref, parts_ref, sums_ref,
):
    rows = self_ref.shape[0]
    density = keep_ref[:rows, :] + got_ref[:rows, :]
    mixed = keep_ref[rows:, :] + got_ref[rows:, :]
    interp = bracket_read(mixed, bracket_ref[1, 0], lam_ref[1, 0])
    tax = tax_ref[1]
    share = energy_ref[0]
    spent = density * (share * lax.rsqrt(interp))
    half = demand_ref.shape[0]
    demand_ref[...] = (scale / (1.0 + tax)) * sum(spent[k : k + half] for k in range(0, rows, half))
    value = gross_rate * interp * (1.0 + tax * share)
    moved = push_assets(density, fwd_bracket_ref[1, 0], fwd_weight_ref[1, 0], parts_ref, sums_ref)
    to_self, to_plus, to_minus = level_shares(moved, step_ref[1, 0], omega_ref[1, 0])
    self_ref[...] = to_self
    value_ref[...] = value
    store_halo(pair_ref, other_ref, to_plus, to_minus, value)


def close_kernel(keep_ref, got_ref, own_ref, *rest):
    (*other_refs, energy_ref, tax_ref, demand_ref, value_ref, mass_ref, terms_ref, out_ref, spent_ref, sems) = rest
    rows = energy_ref.shape[1]
    chip = lax.axis_index("x")
    out_ref[1, 0] = keep_ref[:rows, :] + got_ref[:rows, :]
    mass_copy = pltpu.make_async_copy(out_ref.at[1], mass_ref, sems.at[1])
    mass_copy.start()
    value_copy = pltpu.make_async_copy(out_ref.at[0], value_ref, sems.at[0])
    for shift, ref in zip(SHIFTS, (own_ref, *other_refs)):
        part = pl.ds(pl.multiple_of(((chip ^ shift) + 1) * rows, rows), rows)
        bracket = ref[3 * rows : 4 * rows, :].astype(jnp.int32)
        interp = bracket_read(keep_ref[part, :] + got_ref[part, :], bracket, ref[4 * rows :, :])
        spent_ref[chip ^ shift] = ref[2 * rows : 3 * rows, :] * lax.rsqrt(interp)
        if shift == 0:
            out_ref[0, 0] = gross_rate * interp * (1.0 + tax_ref[0] * energy_ref[0])
            value_copy.start()
    first = jnp.sum((spent_ref[0] + spent_ref[1]) + (spent_ref[2] + spent_ref[3]), axis=(0, 1), keepdims=True)
    second = jnp.sum(demand_ref[...], axis=(0, 1), keepdims=True)
    lane = lax.broadcasted_iota(jnp.int32, (1, LANES), 1)
    terms_ref[...] = jnp.broadcast_to(jnp.where(lane == 0, first, second)[None], terms_ref.shape)
    mass_copy.wait()
    value_copy.wait()


def demand_kernel(terms_ref, out_ref):
    out_ref[...] = jnp.sum(terms_ref[...], axis=0)[0, : out_ref.shape[0]]


def per_device(
    value_next,
    markov,
    energy_share,
    bwd_bracket,
    bwd_weight,
    fwd_bracket,
    fwd_weight,
    dur_step,
    dur_weight,
    mass_start,
    tax,
):
    _, rows, assets = value_next.shape
    states = markov.shape[0]
    levels, chips, cores = (lax.axis_size(axis) for axis in ("dur", "x", "core"))
    scale = 1.0 / (levels * states * assets)
    chunks = assets // (LANES // 2)
    slab = pltpu.VMEM((rows, assets), F32)
    pair = pltpu.VMEM((2 * rows, assets), F32)
    block = jax.ShapeDtypeStruct((1, rows, assets), F32)
    eight = pltpu.VMEM((8, assets), F32)
    push_scratch = [pltpu.VMEM((4, rows, assets), F32), pltpu.VMEM((rows * 4 * chunks, LANES), F32)]
    pairs = [(i, i ^ 1) for i in range(levels)]
    others = [(i, ((i + 1) ^ 1) - 1) for i in range(1, levels - 1)]

    def over_chips(array):
        return [lax.ppermute(array, "x", [(i, i ^ k) for i in range(chips)]) for k in SHIFTS[1:]]

    def over_cores(array):
        return lax.ppermute(array, "core", [(i, i ^ 1) for i in range(cores)])

    def over_levels(pair_out, other_out):
        other_in = lax.ppermute(other_out, "dur", others)
        return other_in, lax.ppermute(pair_out, "dur", pairs)

    weights = pl.pallas_call(
        weights_kernel,
        out_shape=(pltpu.VMEM((2 * states, states), BF16), pltpu.VMEM((4 * rows, states), BF16)),
        in_specs=[VMEM],
        out_specs=(VMEM, VMEM),
        scratch_shapes=[pltpu.VMEM((states, states), F32)],
        name="weights",
    )(*in_vmem(markov))
    pair_out, other_out, kept, fixed = pl.pallas_call(
        functools.partial(open_kernel, scale),
        out_shape=(pair, pair, slab, pltpu.VMEM((3 * rows, assets), F32)),
        in_specs=[VMEM] * 9 + [SMEM],
        out_specs=(VMEM,) * 4,
        scratch_shapes=push_scratch,
        name="open",
    )(
        value_next, mass_start, fwd_bracket, fwd_weight, dur_step, dur_weight, energy_share, bwd_bracket, bwd_weight, tax
    )
    halo = over_levels(pair_out, other_out)
    mine = pl.pallas_call(
        merge_kernel,
        out_shape=pltpu.VMEM((5 * rows, assets), F32),
        in_specs=[VMEM] * 5,
        out_specs=VMEM,
        name="merge_with_fixed",
    )(*in_vmem(kept, value_next, *halo, fixed))
    every_first = [mine] + over_chips(mine)
    keep, send = pl.pallas_call(
        markov_kernel,
        out_shape=(pair, pair),
        in_specs=[VMEM] * 6,
        out_specs=(VMEM, VMEM),
        scratch_shapes=[pltpu.VMEM((states, assets), F32), pltpu.VMEM((2 * rows, assets), F32)],
        name="markov",
    )(*in_vmem(*every_first, *weights))
    pair_out, other_out, kept, value, second = pl.pallas_call(
        functools.partial(turn_kernel, scale),
        out_shape=(pair, pair, slab, slab, eight),
        in_specs=[VMEM] * 5 + [SMEM] + [VMEM] * 4,
        out_specs=(VMEM,) * 5,
        scratch_shapes=push_scratch,
        name="turn",
    )(
        *in_vmem(keep, over_cores(send), bwd_bracket, bwd_weight, energy_share),
        tax,
        *in_vmem(fwd_bracket, fwd_weight, dur_step, dur_weight),
    )
    halo = over_levels(pair_out, other_out)
    mine = pl.pallas_call(
        merge_kernel,
        out_shape=pltpu.VMEM((2 * rows + 8, assets), F32),
        in_specs=[VMEM] * 5,
        out_specs=VMEM,
        name="merge_with_demand",
    )(*in_vmem(kept, value, *halo, second))
    wide = pltpu.VMEM(((1 + chips) * rows, assets), F32)
    keep, send, second = pl.pallas_call(
        markov_wide_kernel,
        out_shape=(wide, wide, eight),
        in_specs=[VMEM] * 6,
        out_specs=(VMEM,) * 3,
        scratch_shapes=[
            pltpu.VMEM((states, assets), F32),
            pltpu.VMEM((states, assets), F32),
            pltpu.VMEM((chips, 8, assets), F32),
        ],
        name="markov_wide",
    )(*in_vmem(mine, *over_chips(mine), *weights))
    value_start, mass_end, terms = pl.pallas_call(
        close_kernel,
        out_shape=(block, block, pltpu.VMEM((levels * cores, 1, LANES), F32)),
        in_specs=[VMEM] * 7 + [SMEM, VMEM],
        out_specs=(pl.BlockSpec(memory_space=pl.ANY),) * 2 + (VMEM,),
        scratch_shapes=[
            pltpu.VMEM((2, 1, rows, assets), F32),
            pltpu.VMEM((chips, rows, assets), F32),
            pltpu.SemaphoreType.DMA((2,)),
        ],
        name="close",
    )(*in_vmem(keep, over_cores(send), *every_first, energy_share), tax, *in_vmem(second))
    every_term = lax.all_to_all(terms, ("dur", "core"), 0, 0)
    demand = pl.pallas_call(
        demand_kernel,
        out_shape=jax.ShapeDtypeStruct((2,), F32),
        in_specs=[VMEM],
        out_specs=VMEM,
        name="demand",
    )(*in_vmem(every_term))
    return (value_start, mass_end, demand)


def solution(mesh):
    levels, incs = mesh.devices.shape
    mesh = Mesh(mesh.devices.reshape(levels, incs // 2, 2), ("dur", "x", "core"))
    inc = ("x", "core")
    return jax.shard_map(
        per_device,
        mesh=mesh,
        in_specs=(
            P("dur", inc, None),
            P(),
            P("dur", inc, None),
            P(None, "dur", inc, None),
            P(None, "dur", inc, None),
            P(None, "dur", inc, None),
            P(None, "dur", inc, None),
            P(None, "dur", inc, None),
            P(None, "dur", inc, None),
            P("dur", inc, None),
            P(),
        ),
        out_specs=(P("dur", inc, None), P("dur", inc, None), P()),
        check_vma=False,
    )
```

```python
import functools

import jax
import jax.numpy as jnp
from jax import lax
from jax.experimental import pallas as pl
from jax.experimental.pallas import tpu as pltpu
from jax.sharding import Mesh, PartitionSpec as P

discount = 0.985
gross_rate = 1.01
adjust_share = 0.3

LANES = 128
SHIFTS = (0, 1, 3, 2)
F32 = jnp.float32
BF16 = jnp.bfloat16
VMEM = pl.BlockSpec(memory_space=pltpu.VMEM)
SMEM = pl.BlockSpec(memory_space=pltpu.SMEM)


def in_vmem(*arrays):
    return tuple(pltpu.with_memory_space_constraint(x, pltpu.VMEM) for x in arrays)


def split_bf16(x):
    high = x.astype(BF16)
    return high, (x - high.astype(F32)).astype(BF16)


def bracket_read(mixed, bracket, weight):
    rows, assets = mixed.shape
    chunks = assets // LANES
    upper = pltpu.roll(mixed, assets - 1, 1)
    chunk_of = bracket >> (LANES.bit_length() - 1)
    lane_of = bracket & (LANES - 1)

    def chosen(values, chunk, first):
        if len(values) == 1:
            return values[0]
        half = len(values) // 2
        return jnp.where(
            chunk < first + half, chosen(values[:half], chunk, first), chosen(values[half:], chunk, first + half)
        )

    groups = []
    for top in range(0, rows, 8):
        part = slice(top, top + 8)
        pieces = []
        for out in range(chunks):
            span = slice(out * LANES, (out + 1) * LANES)
            lane, chunk, lam = lane_of[part, span], chunk_of[part, span], weight[part, span]
            low, high = (
                chosen(
                    [
                        jnp.take_along_axis(
                            table[part, k * LANES : (k + 1) * LANES], lane, axis=1, mode="promise_in_bounds"
                        )
                        for k in range(chunks)
                    ],
                    chunk,
                    0,
                )
                for table in (mixed, upper)
            )
            pieces.append((1.0 - lam) * low + lam * high)
        groups.append(jnp.concatenate(pieces, axis=1))
    return jnp.concatenate(groups, axis=0)


def push_assets(density, bracket, weight, parts_ref, sums_ref):
    rows, assets = density.shape
    width = LANES // 2
    chunks = assets // width
    chunk_of = bracket >> (width.bit_length() - 1)
    place_of = bracket & (width - 1)
    share = weight * density
    for k, value in enumerate((density - share, share)):
        high, low = split_bf16(value)
        parts_ref[2 * k] = high.astype(F32)
        parts_ref[2 * k + 1] = low.astype(F32)
    height = 4 * chunks
    chunk_iota = lax.broadcasted_iota(jnp.int32, (chunks, assets), 0)
    place_iota = lax.broadcasted_iota(jnp.int32, (width, assets), 0)
    for r in range(rows):
        row = slice(r, r + 1)
        here = chunk_iota == chunk_of[row, :]
        left = jnp.concatenate([jnp.where(here, parts_ref[k, row, :], 0.0) for k in range(4)], axis=0).astype(BF16)
        right = jnp.where(place_iota == place_of[row, :], 1.0, 0.0).astype(BF16)
        sums_ref[r * height : (r + 1) * height, :width] = lax.dot_general(
            left, right, (((1,), (1,)), ((), ())), preferred_element_type=F32
        )
    low_half = lax.broadcasted_iota(jnp.int32, (rows, LANES), 1) < width

    def gathered(k, h):
        high, low = (sums_ref[pl.ds((k + term) * chunks + h, rows, stride=height), :] for term in range(2))
        return high + low

    def assembled(k):
        return jnp.concatenate(
            [
                jnp.where(low_half, gathered(k, h), pltpu.roll(gathered(k, h + 1), width, 1))
                for h in range(0, chunks, 2)
            ],
            axis=1,
        )

    return assembled(0) + pltpu.roll(assembled(2), 1, 1)


def level_shares(moved, step, omega):
    level = lax.axis_index("dur")
    total = lax.axis_size("dur")
    lower = jnp.clip(level + step, 0, total - 2)
    down = lower - level == -1
    upper_part = moved * omega
    lower_part = moved - upper_part
    to_self = jnp.where(down, upper_part, lower_part)
    to_minus = jnp.where(down, lower_part, 0.0)
    to_plus = jnp.where(down, 0.0, upper_part)
    return to_self, to_plus, to_minus


def store_halo(pair_ref, other_ref, to_plus, to_minus, value):
    rows = value.shape[0]
    even = lax.axis_index("dur") % 2 == 0
    pair_ref[:rows, :] = jnp.where(even, to_plus, to_minus)
    other_ref[:rows, :] = jnp.where(even, to_minus, to_plus)
    pair_ref[rows:, :] = value
    other_ref[rows:, :] = value


def weights_kernel(markov_ref, tax_ref, back_ref, ahead_ref, rates_ref, flip_ref):
    for quarter in range(2):
        rates_ref[quarter : quarter + 1, :] = jnp.full((1, LANES), tax_ref[quarter], F32)
    chip = lax.axis_index("x")
    states = markov_ref.shape[0]
    wide = ahead_ref.shape[0] // 2
    flip_ref[...] = markov_ref[...].T
    high, low = split_bf16(discount * markov_ref[...])
    back_ref[:states, :] = high
    back_ref[states:, :] = low
    high, low = split_bf16(flip_ref[pl.ds(pl.multiple_of(chip * wide, wide), wide), :])
    ahead_ref[:wide, :] = high
    ahead_ref[wide:, :] = low


def fixed_kernel(scale, energy_ref, mass_ref, bracket_ref, lam_ref, tax_ref, out_ref):
    rows = energy_ref.shape[1]
    out_ref[:rows, :] = scale * mass_ref[0] * energy_ref[0] / (1.0 + tax_ref[0])
    out_ref[rows : 2 * rows, :] = bracket_ref[0, 0].astype(F32)
    out_ref[2 * rows :, :] = lam_ref[0, 0]


def open_kernel(
    value_ref, mass_ref, bracket_ref, weight_ref, step_ref, omega_ref, pair_ref, other_ref, self_ref, parts_ref, sums_ref
):
    moved = push_assets(mass_ref[0], bracket_ref[0, 0], weight_ref[0, 0], parts_ref, sums_ref)
    to_self, to_plus, to_minus = level_shares(moved, step_ref[0, 0], omega_ref[0, 0])
    self_ref[...] = to_self
    store_halo(pair_ref, other_ref, to_plus, to_minus, value_ref[0])


def merge_kernel(self_ref, value_ref, other_ref, pair_ref, rider_ref, out_ref):
    rows = self_ref.shape[0]
    level = lax.axis_index("dur")
    value = value_ref[...].reshape(self_ref.shape)
    alone = (level == 0) | (level == lax.axis_size("dur") - 1)
    beside = pair_ref[rows:, :] + jnp.where(alone, value, other_ref[rows:, :])
    incoming = pair_ref[:rows, :] + jnp.where(alone, 0.0, other_ref[:rows, :])
    out_ref[:rows, :] = self_ref[...] + incoming
    out_ref[rows : 2 * rows, :] = (1.0 - adjust_share) * value + adjust_share * 0.5 * beside
    out_ref[2 * rows :, :] = rider_ref[...]


def place_field(refs, part, rows, field_ref):
    chip, core = lax.axis_index("x"), lax.axis_index("core")
    field_ref[...] = jnp.zeros_like(field_ref)
    for shift, ref in zip(SHIFTS, refs):
        at = pl.ds(pl.multiple_of((chip ^ shift) * 2 * rows + core * rows, rows), rows)
        field_ref[at, :] = ref[part * rows : (part + 1) * rows, :]
    return split_bf16(field_ref[...])


def product(factor_high, factor_low, high, low):
    count = factor_high.shape[0]
    both = jnp.dot(jnp.concatenate([factor_high, factor_low], axis=0), high, preferred_element_type=F32)
    return both[:count] + (both[count:] + jnp.dot(factor_high, low, preferred_element_type=F32))


def markov_kernel(
    own_ref, one_ref, two_ref, three_ref, back_ref, ahead_ref, keep_ref, send_ref, field_ref, total_ref
):
    refs = (own_ref, one_ref, two_ref, three_ref)
    chip, core = lax.axis_index("x"), lax.axis_index("core")
    states = back_ref.shape[0] // 2
    wide = ahead_ref.shape[0] // 2
    rows = wide // 2
    mine = pl.ds(pl.multiple_of(core * rows, rows), rows)
    theirs = pl.ds(pl.multiple_of((1 - core) * rows, rows), rows)
    total_ref[:wide, :] = product(ahead_ref[:wide, :], ahead_ref[wide:, :], *place_field(refs, 0, rows, field_ref))
    keep_ref[:rows, :] = total_ref[mine, :]
    send_ref[:rows, :] = total_ref[theirs, :]
    at = pl.multiple_of(chip * wide, wide)
    total_ref[:wide, :] = product(
        back_ref[pl.ds(at, wide), :],
        back_ref[pl.ds(states + at, wide), :],
        *place_field(refs, 1, rows, field_ref),
    )
    keep_ref[rows:, :] = total_ref[mine, :]
    send_ref[rows:, :] = total_ref[theirs, :]


def markov_wide_kernel(
    own_ref, one_ref, two_ref, three_ref, back_ref, ahead_ref, keep_ref, send_ref, demand_ref, field_ref, total_ref,
    terms_ref,
):
    refs = (own_ref, one_ref, two_ref, three_ref)
    chip, core = lax.axis_index("x"), lax.axis_index("core")
    states = back_ref.shape[0] // 2
    wide = ahead_ref.shape[0] // 2
    rows = wide // 2
    mine = pl.ds(pl.multiple_of(core * rows, rows), rows)
    theirs = pl.ds(pl.multiple_of((1 - core) * rows, rows), rows)
    total_ref[:wide, :] = product(ahead_ref[:wide, :], ahead_ref[wide:, :], *place_field(refs, 0, rows, field_ref))
    keep_ref[:rows, :] = total_ref[mine, :]
    send_ref[:rows, :] = total_ref[theirs, :]
    total_ref[...] = product(back_ref[:states, :], back_ref[states:, :], *place_field(refs, 1, rows, field_ref))
    for k in range(len(refs)):
        part = slice((k + 1) * rows, (k + 2) * rows)
        keep_ref[part, :] = total_ref[pl.ds(pl.multiple_of(k * wide + core * rows, rows), rows), :]
        send_ref[part, :] = total_ref[pl.ds(pl.multiple_of(k * wide + (1 - core) * rows, rows), rows), :]
    for shift, ref in zip(SHIFTS, refs):
        terms_ref[chip ^ shift] = ref[2 * rows :, :]
    demand_ref[...] = (terms_ref[0] + terms_ref[1]) + (terms_ref[2] + terms_ref[3])


def turn_kernel(
    scale, keep_ref, got_ref, bracket_ref, lam_ref, energy_ref, rates_ref, fwd_bracket_ref, fwd_weight_ref, step_ref,
    omega_ref, pair_ref, other_ref, self_ref, value_ref, demand_ref, parts_ref, sums_ref,
):
    rows = self_ref.shape[0]
    density = keep_ref[:rows, :] + got_ref[:rows, :]
    mixed = keep_ref[rows:, :] + got_ref[rows:, :]
    interp = bracket_read(mixed, bracket_ref[1, 0], lam_ref[1, 0])
    tax = rates_ref[1:2, :1]
    share = energy_ref[0]
    spent = density * (share * lax.rsqrt(interp))
    half = demand_ref.shape[0]
    demand_ref[...] = (scale / (1.0 + tax)) * sum(spent[k : k + half] for k in range(0, rows, half))
    value = gross_rate * interp * (1.0 + tax * share)
    moved = push_assets(density, fwd_bracket_ref[1, 0], fwd_weight_ref[1, 0], parts_ref, sums_ref)
    to_self, to_plus, to_minus = level_shares(moved, step_ref[1, 0], omega_ref[1, 0])
    self_ref[...] = to_self
    value_ref[...] = value
    store_halo(pair_ref, other_ref, to_plus, to_minus, value)


def folded(terms):
    return sum(
        terms[top : top + 8, left : left + LANES]
        for top in range(0, terms.shape[0], 8)
        for left in range(0, terms.shape[1], LANES)
    )


def close_kernel(keep_ref, got_ref, own_ref, *rest):
    (*other_refs, energy_ref, rates_ref, demand_ref, value_ref, mass_ref, terms_ref, out_ref, spent_ref, sems) = rest
    rows = energy_ref.shape[1]
    chip = lax.axis_index("x")
    out_ref[1, 0] = keep_ref[:rows, :] + got_ref[:rows, :]
    mass_copy = pltpu.make_async_copy(out_ref.at[1], mass_ref, sems.at[1])
    mass_copy.start()
    value_copy = pltpu.make_async_copy(out_ref.at[0], value_ref, sems.at[0])
    for shift, ref in zip(SHIFTS, (own_ref, *other_refs)):
        part = pl.ds(pl.multiple_of(((chip ^ shift) + 1) * rows, rows), rows)
        bracket = ref[3 * rows : 4 * rows, :].astype(jnp.int32)
        interp = bracket_read(keep_ref[part, :] + got_ref[part, :], bracket, ref[4 * rows :, :])
        spent = ref[2 * rows : 3 * rows, :] * lax.rsqrt(interp)
        spent_ref[chip ^ shift] = folded(spent)
        if shift == 0:
            out_ref[0, 0] = gross_rate * interp * (1.0 + rates_ref[:1, :1] * energy_ref[0])
            value_copy.start()
    first = jnp.sum((spent_ref[0] + spent_ref[1]) + (spent_ref[2] + spent_ref[3]), axis=(0, 1), keepdims=True)
    second = jnp.sum(folded(demand_ref[...]), axis=(0, 1), keepdims=True)
    lane = lax.broadcasted_iota(jnp.int32, (1, LANES), 1)
    terms_ref[...] = jnp.broadcast_to(jnp.where(lane == 0, first, second)[None], terms_ref.shape)
    mass_copy.wait()
    value_copy.wait()


def demand_kernel(terms_ref, out_ref):
    out_ref[...] = jnp.sum(terms_ref[...], axis=0)[0, : out_ref.shape[0]]


def per_device(
    value_next,
    markov,
    energy_share,
    bwd_bracket,
    bwd_weight,
    fwd_bracket,
    fwd_weight,
    dur_step,
    dur_weight,
    mass_start,
    tax,
):
    _, rows, assets = value_next.shape
    states = markov.shape[0]
    levels, chips, cores = (lax.axis_size(axis) for axis in ("dur", "x", "core"))
    scale = 1.0 / (levels * states * assets)
    chunks = assets // (LANES // 2)
    slab = pltpu.VMEM((rows, assets), F32)
    pair = pltpu.VMEM((2 * rows, assets), F32)
    block = jax.ShapeDtypeStruct((1, rows, assets), F32)
    eight = pltpu.VMEM((8, assets), F32)
    push_scratch = [pltpu.VMEM((4, rows, assets), F32), pltpu.VMEM((rows * 4 * chunks, LANES), F32)]
    pairs = [(i, i ^ 1) for i in range(levels)]
    others = [(i, ((i + 1) ^ 1) - 1) for i in range(1, levels - 1)]

    def over_chips(array):
        return [lax.ppermute(array, "x", [(i, i ^ k) for i in range(chips)]) for k in SHIFTS[1:]]

    def over_cores(array):
        return lax.ppermute(array, "core", [(i, i ^ 1) for i in range(cores)])

    def over_levels(pair_out, other_out):
        other_in = lax.ppermute(other_out, "dur", others)
        return other_in, lax.ppermute(pair_out, "dur", pairs)

    *weights, rates = pl.pallas_call(
        weights_kernel,
        out_shape=(
            pltpu.VMEM((2 * states, states), BF16),
            pltpu.VMEM((4 * rows, states), BF16),
            pltpu.VMEM((8, LANES), F32),
        ),
        in_specs=[VMEM, SMEM],
        out_specs=(VMEM,) * 3,
        scratch_shapes=[pltpu.VMEM((states, states), F32)],
        name="weights",
    )(*in_vmem(markov), tax)
    fixed = pl.pallas_call(
        functools.partial(fixed_kernel, scale),
        out_shape=pltpu.VMEM((3 * rows, assets), F32),
        in_specs=[VMEM] * 4 + [SMEM],
        out_specs=VMEM,
        name="fixed",
    )(*in_vmem(energy_share, mass_start, bwd_bracket, bwd_weight), tax)
    pair_out, other_out, kept = pl.pallas_call(
        open_kernel,
        out_shape=(pair, pair, slab),
        in_specs=[VMEM] * 6,
        out_specs=(VMEM,) * 3,
        scratch_shapes=push_scratch,
        name="open",
    )(value_next, mass_start, fwd_bracket, fwd_weight, dur_step, dur_weight)
    halo = over_levels(pair_out, other_out)
    mine = pl.pallas_call(
        merge_kernel,
        out_shape=pltpu.VMEM((5 * rows, assets), F32),
        in_specs=[VMEM] * 5,
        out_specs=VMEM,
        name="merge_with_fixed",
    )(*in_vmem(kept, value_next, *halo, fixed))
    every_first = [mine] + over_chips(mine)
    keep, send = pl.pallas_call(
        markov_kernel,
        out_shape=(pair, pair),
        in_specs=[VMEM] * 6,
        out_specs=(VMEM, VMEM),
        scratch_shapes=[pltpu.VMEM((states, assets), F32), pltpu.VMEM((2 * rows, assets), F32)],
        name="markov",
    )(*in_vmem(*every_first, *weights))
    pair_out, other_out, kept, value, second = pl.pallas_call(
        functools.partial(turn_kernel, scale),
        out_shape=(pair, pair, slab, slab, eight),
        in_specs=[VMEM] * 10,
        out_specs=(VMEM,) * 5,
        scratch_shapes=push_scratch,
        name="turn",
    )(
        *in_vmem(keep, over_cores(send), bwd_bracket, bwd_weight, energy_share, rates),
        *in_vmem(fwd_bracket, fwd_weight, dur_step, dur_weight),
    )
    halo = over_levels(pair_out, other_out)
    mine = pl.pallas_call(
        merge_kernel,
        out_shape=pltpu.VMEM((2 * rows + 8, assets), F32),
        in_specs=[VMEM] * 5,
        out_specs=VMEM,
        name="merge_with_demand",
    )(*in_vmem(kept, value, *halo, second))
    wide = pltpu.VMEM(((1 + chips) * rows, assets), F32)
    keep, send, second = pl.pallas_call(
        markov_wide_kernel,
        out_shape=(wide, wide, eight),
        in_specs=[VMEM] * 6,
        out_specs=(VMEM,) * 3,
        scratch_shapes=[
            pltpu.VMEM((states, assets), F32),
            pltpu.VMEM((states, assets), F32),
            pltpu.VMEM((chips, 8, assets), F32),
        ],
        name="markov_wide",
    )(*in_vmem(mine, *over_chips(mine), *weights))
    value_start, mass_end, terms = pl.pallas_call(
        close_kernel,
        out_shape=(block, block, pltpu.VMEM((levels * cores, 1, LANES), F32)),
        in_specs=[VMEM] * 9,
        out_specs=(pl.BlockSpec(memory_space=pl.ANY),) * 2 + (VMEM,),
        scratch_shapes=[
            pltpu.VMEM((2, 1, rows, assets), F32),
            pltpu.VMEM((chips, 8, LANES), F32),
            pltpu.SemaphoreType.DMA((2,)),
        ],
        name="close",
    )(*in_vmem(keep, over_cores(send), *every_first, energy_share, rates, second))
    every_term = lax.all_to_all(terms, ("dur", "core"), 0, 0)
    demand = pl.pallas_call(
        demand_kernel,
        out_shape=jax.ShapeDtypeStruct((2,), F32),
        in_specs=[VMEM],
        out_specs=VMEM,
        name="demand",
    )(*in_vmem(every_term))
    return (value_start, mass_end, demand)


def solution(mesh):
    levels, incs = mesh.devices.shape
    mesh = Mesh(mesh.devices.reshape(levels, incs // 2, 2), ("dur", "x", "core"))
    inc = ("x", "core")
    return jax.shard_map(
        per_device,
        mesh=mesh,
        in_specs=(
            P("dur", inc, None),
            P(),
            P("dur", inc, None),
            P(None, "dur", inc, None),
            P(None, "dur", inc, None),
            P(None, "dur", inc, None),
            P(None, "dur", inc, None),
            P(None, "dur", inc, None),
            P(None, "dur", inc, None),
            P("dur", inc, None),
            P(),
        ),
        out_specs=(P("dur", inc, None), P("dur", inc, None), P()),
        check_vma=False,
    )
```

```python
import functools

import jax
import jax.numpy as jnp
from jax import lax
from jax.experimental import pallas as pl
from jax.experimental.pallas import tpu as pltpu
from jax.sharding import Mesh, PartitionSpec as P

discount = 0.985
gross_rate = 1.01
adjust_share = 0.3

LANES = 128
SHIFTS = (0, 1, 3, 2)
F32 = jnp.float32
BF16 = jnp.bfloat16
VMEM = pl.BlockSpec(memory_space=pltpu.VMEM)


def in_vmem(*arrays):
    return tuple(pltpu.with_memory_space_constraint(x, pltpu.VMEM) for x in arrays)


def split_bf16(x):
    high = x.astype(BF16)
    return high, (x - high.astype(F32)).astype(BF16)


def bracket_read(mixed, bracket, weight):
    rows, assets = mixed.shape
    chunks = assets // LANES
    upper = pltpu.roll(mixed, assets - 1, 1)
    chunk_of = bracket >> (LANES.bit_length() - 1)
    lane_of = bracket & (LANES - 1)

    def chosen(values, chunk, first):
        if len(values) == 1:
            return values[0]
        half = len(values) // 2
        return jnp.where(
            chunk < first + half, chosen(values[:half], chunk, first), chosen(values[half:], chunk, first + half)
        )

    groups = []
    for top in range(0, rows, 8):
        part = slice(top, top + 8)
        pieces = []
        for out in range(chunks):
            span = slice(out * LANES, (out + 1) * LANES)
            lane, chunk, lam = lane_of[part, span], chunk_of[part, span], weight[part, span]
            low, high = (
                chosen(
                    [
                        jnp.take_along_axis(
                            table[part, k * LANES : (k + 1) * LANES], lane, axis=1, mode="promise_in_bounds"
                        )
                        for k in range(chunks)
                    ],
                    chunk,
                    0,
                )
                for table in (mixed, upper)
            )
            pieces.append((1.0 - lam) * low + lam * high)
        groups.append(jnp.concatenate(pieces, axis=1))
    return jnp.concatenate(groups, axis=0)


def push_assets(density, bracket, weight, parts_ref, sums_ref):
    rows, assets = density.shape
    width = LANES // 2
    chunks = assets // width
    chunk_of = bracket >> (width.bit_length() - 1)
    place_of = bracket & (width - 1)
    share = weight * density
    for k, value in enumerate((density - share, share)):
        high, low = split_bf16(value)
        parts_ref[2 * k] = high.astype(F32)
        parts_ref[2 * k + 1] = low.astype(F32)
    height = 4 * chunks
    chunk_iota = lax.broadcasted_iota(jnp.int32, (chunks, assets), 0)
    place_iota = lax.broadcasted_iota(jnp.int32, (width, assets), 0)
    for r in range(rows):
        row = slice(r, r + 1)
        here = chunk_iota == chunk_of[row, :]
        left = jnp.concatenate([jnp.where(here, parts_ref[k, row, :], 0.0) for k in range(4)], axis=0).astype(BF16)
        right = jnp.where(place_iota == place_of[row, :], 1.0, 0.0).astype(BF16)
        sums_ref[r * height : (r + 1) * height, :width] = lax.dot_general(
            left, right, (((1,), (1,)), ((), ())), preferred_element_type=F32
        )
    low_half = lax.broadcasted_iota(jnp.int32, (rows, LANES), 1) < width

    def gathered(k, h):
        high, low = (sums_ref[pl.ds((k + term) * chunks + h, rows, stride=height), :] for term in range(2))
        return high + low

    def assembled(k):
        return jnp.concatenate(
            [
                jnp.where(low_half, gathered(k, h), pltpu.roll(gathered(k, h + 1), width, 1))
                for h in range(0, chunks, 2)
            ],
            axis=1,
        )

    return assembled(0) + pltpu.roll(assembled(2), 1, 1)


def level_shares(moved, step, omega):
    level = lax.axis_index("dur")
    total = lax.axis_size("dur")
    lower = jnp.clip(level + step, 0, total - 2)
    down = lower - level == -1
    upper_part = moved * omega
    lower_part = moved - upper_part
    to_self = jnp.where(down, upper_part, lower_part)
    to_minus = jnp.where(down, lower_part, 0.0)
    to_plus = jnp.where(down, 0.0, upper_part)
    return to_self, to_plus, to_minus


def store_halo(pair_ref, other_ref, to_plus, to_minus, value):
    rows = value.shape[0]
    even = lax.axis_index("dur") % 2 == 0
    pair_ref[:rows, :] = jnp.where(even, to_plus, to_minus)
    other_ref[:rows, :] = jnp.where(even, to_minus, to_plus)
    pair_ref[rows:, :] = value
    other_ref[rows:, :] = value


def weights_kernel(markov_ref, tax_ref, back_ref, ahead_ref, rates_ref, flip_ref):
    taxes = tax_ref[...].reshape(1, 2)
    for quarter in range(2):
        tax = jnp.broadcast_to(taxes[:, quarter : quarter + 1], (1, LANES))
        rates_ref[quarter : quarter + 1, :] = tax
        rates_ref[2 + quarter : 3 + quarter, :] = 1.0 / (1.0 + tax)
    chip = lax.axis_index("x")
    states = markov_ref.shape[0]
    wide = ahead_ref.shape[0] // 2
    flip_ref[...] = markov_ref[...].T
    high, low = split_bf16(discount * markov_ref[...])
    back_ref[:states, :] = high
    back_ref[states:, :] = low
    high, low = split_bf16(flip_ref[pl.ds(pl.multiple_of(chip * wide, wide), wide), :])
    ahead_ref[:wide, :] = high
    ahead_ref[wide:, :] = low


def fixed_kernel(scale, energy_ref, mass_ref, bracket_ref, out_ref):
    rows = energy_ref.shape[1]
    out_ref[:rows, :] = scale * mass_ref[0] * energy_ref[0]
    out_ref[rows:, :] = bracket_ref[0, 0].astype(F32)


def open_kernel(
    value_ref, mass_ref, bracket_ref, weight_ref, step_ref, omega_ref, pair_ref, other_ref, self_ref, parts_ref, sums_ref
):
    moved = push_assets(mass_ref[0], bracket_ref[0, 0], weight_ref[0, 0], parts_ref, sums_ref)
    to_self, to_plus, to_minus = level_shares(moved, step_ref[0, 0], omega_ref[0, 0])
    self_ref[...] = to_self
    store_halo(pair_ref, other_ref, to_plus, to_minus, value_ref[0])


def merge_kernel(self_ref, value_ref, other_ref, pair_ref, *rest):
    *rider_refs, out_ref = rest
    rows = self_ref.shape[0]
    level = lax.axis_index("dur")
    value = value_ref[...].reshape(self_ref.shape)
    alone = (level == 0) | (level == lax.axis_size("dur") - 1)
    beside = pair_ref[rows:, :] + jnp.where(alone, value, other_ref[rows:, :])
    incoming = pair_ref[:rows, :] + jnp.where(alone, 0.0, other_ref[:rows, :])
    out_ref[:rows, :] = self_ref[...] + incoming
    out_ref[rows : 2 * rows, :] = (1.0 - adjust_share) * value + adjust_share * 0.5 * beside
    top = 2 * rows
    for ref in rider_refs:
        rider = ref[0, 0] if len(ref.shape) == 4 else ref[...]
        out_ref[top : top + rider.shape[0], :] = rider
        top += rider.shape[0]


def place_field(refs, part, rows, field_ref):
    chip, core = lax.axis_index("x"), lax.axis_index("core")
    field_ref[...] = jnp.zeros_like(field_ref)
    for shift, ref in zip(SHIFTS, refs):
        at = pl.ds(pl.multiple_of((chip ^ shift) * 2 * rows + core * rows, rows), rows)
        field_ref[at, :] = ref[part * rows : (part + 1) * rows, :]
    return split_bf16(field_ref[...])


def product(factor_high, factor_low, high, low):
    count = factor_high.shape[0]
    both = jnp.dot(jnp.concatenate([factor_high, factor_low], axis=0), high, preferred_element_type=F32)
    return both[:count] + (both[count:] + jnp.dot(factor_high, low, preferred_element_type=F32))


def markov_kernel(
    own_ref, one_ref, two_ref, three_ref, back_ref, ahead_ref, keep_ref, send_ref, field_ref, total_ref
):
    refs = (own_ref, one_ref, two_ref, three_ref)
    chip, core = lax.axis_index("x"), lax.axis_index("core")
    states = back_ref.shape[0] // 2
    wide = ahead_ref.shape[0] // 2
    rows = wide // 2
    mine = pl.ds(pl.multiple_of(core * rows, rows), rows)
    theirs = pl.ds(pl.multiple_of((1 - core) * rows, rows), rows)
    total_ref[:wide, :] = product(ahead_ref[:wide, :], ahead_ref[wide:, :], *place_field(refs, 0, rows, field_ref))
    keep_ref[:rows, :] = total_ref[mine, :]
    send_ref[:rows, :] = total_ref[theirs, :]
    at = pl.multiple_of(chip * wide, wide)
    total_ref[:wide, :] = product(
        back_ref[pl.ds(at, wide), :],
        back_ref[pl.ds(states + at, wide), :],
        *place_field(refs, 1, rows, field_ref),
    )
    keep_ref[rows:, :] = total_ref[mine, :]
    send_ref[rows:, :] = total_ref[theirs, :]


def markov_wide_kernel(
    own_ref, one_ref, two_ref, three_ref, back_ref, ahead_ref, keep_ref, send_ref, demand_ref, field_ref, total_ref,
    terms_ref,
):
    refs = (own_ref, one_ref, two_ref, three_ref)
    chip, core = lax.axis_index("x"), lax.axis_index("core")
    states = back_ref.shape[0] // 2
    wide = ahead_ref.shape[0] // 2
    rows = wide // 2
    mine = pl.ds(pl.multiple_of(core * rows, rows), rows)
    theirs = pl.ds(pl.multiple_of((1 - core) * rows, rows), rows)
    total_ref[:wide, :] = product(ahead_ref[:wide, :], ahead_ref[wide:, :], *place_field(refs, 0, rows, field_ref))
    keep_ref[:rows, :] = total_ref[mine, :]
    send_ref[:rows, :] = total_ref[theirs, :]
    total_ref[...] = product(back_ref[:states, :], back_ref[states:, :], *place_field(refs, 1, rows, field_ref))
    for k in range(len(refs)):
        part = slice((k + 1) * rows, (k + 2) * rows)
        keep_ref[part, :] = total_ref[pl.ds(pl.multiple_of(k * wide + core * rows, rows), rows), :]
        send_ref[part, :] = total_ref[pl.ds(pl.multiple_of(k * wide + (1 - core) * rows, rows), rows), :]
    for shift, ref in zip(SHIFTS, refs):
        terms_ref[chip ^ shift] = ref[2 * rows : 2 * rows + demand_ref.shape[0], :]
    demand_ref[...] = (terms_ref[0] + terms_ref[1]) + (terms_ref[2] + terms_ref[3])


def turn_kernel(
    scale, keep_ref, got_ref, bracket_ref, lam_ref, energy_ref, rates_ref, fwd_bracket_ref, fwd_weight_ref, step_ref,
    omega_ref, pair_ref, other_ref, self_ref, value_ref, demand_ref, parts_ref, sums_ref,
):
    rows = self_ref.shape[0]
    density = keep_ref[:rows, :] + got_ref[:rows, :]
    mixed = keep_ref[rows:, :] + got_ref[rows:, :]
    interp = bracket_read(mixed, bracket_ref[1, 0], lam_ref[1, 0])
    tax = rates_ref[1:2, :1]
    share = energy_ref[0]
    spent = density * (share * lax.rsqrt(interp))
    half = demand_ref.shape[0]
    demand_ref[...] = (scale * rates_ref[3:4, :1]) * sum(spent[k : k + half] for k in range(0, rows, half))
    value = gross_rate * interp * (1.0 + tax * share)
    moved = push_assets(density, fwd_bracket_ref[1, 0], fwd_weight_ref[1, 0], parts_ref, sums_ref)
    to_self, to_plus, to_minus = level_shares(moved, step_ref[1, 0], omega_ref[1, 0])
    self_ref[...] = to_self
    value_ref[...] = value
    store_halo(pair_ref, other_ref, to_plus, to_minus, value)


def folded(terms):
    return sum(
        terms[top : top + 8, left : left + LANES]
        for top in range(0, terms.shape[0], 8)
        for left in range(0, terms.shape[1], LANES)
    )


def close_kernel(keep_ref, got_ref, *rest):
    (*rider_refs, energy_ref, rates_ref, demand_ref, value_ref, mass_ref, terms_ref, out_ref, spent_ref, sems) = rest
    rows = energy_ref.shape[1]
    chip = lax.axis_index("x")
    tax, shrink = rates_ref[:1, :1], rates_ref[2:3, :1]
    out_ref[1, 0] = keep_ref[:rows, :] + got_ref[:rows, :]
    mass_copy = pltpu.make_async_copy(out_ref.at[1], mass_ref, sems.at[1])
    mass_copy.start()
    value_copy = pltpu.make_async_copy(out_ref.at[0], value_ref, sems.at[0])
    for shift, ref, later_ref in zip(SHIFTS, rider_refs[: len(SHIFTS)], rider_refs[len(SHIFTS) :]):
        part = pl.ds(pl.multiple_of(((chip ^ shift) + 1) * rows, rows), rows)
        bracket = ref[3 * rows : 4 * rows, :].astype(jnp.int32)
        interp = bracket_read(keep_ref[part, :] + got_ref[part, :], bracket, later_ref[later_ref.shape[0] - rows :, :])
        spent = ref[2 * rows : 3 * rows, :] * lax.rsqrt(interp)
        spent_ref[chip ^ shift] = folded(spent)
        if shift == 0:
            out_ref[0, 0] = gross_rate * interp * (1.0 + tax * energy_ref[0])
            value_copy.start()
    first = jnp.sum((spent_ref[0] + spent_ref[1]) + (spent_ref[2] + spent_ref[3]), axis=(0, 1), keepdims=True)
    first = first * shrink
    second = jnp.sum(folded(demand_ref[...]), axis=(0, 1), keepdims=True)
    lane = lax.broadcasted_iota(jnp.int32, (1, LANES), 1)
    terms_ref[...] = jnp.broadcast_to(jnp.where(lane == 0, first, second)[None], terms_ref.shape)
    mass_copy.wait()
    value_copy.wait()


def demand_kernel(terms_ref, out_ref):
    out_ref[...] = jnp.sum(terms_ref[...], axis=0)[0, : out_ref.shape[0]]


def per_device(
    value_next,
    markov,
    energy_share,
    bwd_bracket,
    bwd_weight,
    fwd_bracket,
    fwd_weight,
    dur_step,
    dur_weight,
    mass_start,
    tax,
):
    _, rows, assets = value_next.shape
    states = markov.shape[0]
    levels, chips, cores = (lax.axis_size(axis) for axis in ("dur", "x", "core"))
    scale = 1.0 / (levels * states * assets)
    chunks = assets // (LANES // 2)
    slab = pltpu.VMEM((rows, assets), F32)
    pair = pltpu.VMEM((2 * rows, assets), F32)
    block = jax.ShapeDtypeStruct((1, rows, assets), F32)
    eight = pltpu.VMEM((8, assets), F32)
    push_scratch = [pltpu.VMEM((4, rows, assets), F32), pltpu.VMEM((rows * 4 * chunks, LANES), F32)]
    pairs = [(i, i ^ 1) for i in range(levels)]
    others = [(i, ((i + 1) ^ 1) - 1) for i in range(1, levels - 1)]

    def over_chips(array):
        return [lax.ppermute(array, "x", [(i, i ^ k) for i in range(chips)]) for k in SHIFTS[1:]]

    def over_cores(array):
        return lax.ppermute(array, "core", [(i, i ^ 1) for i in range(cores)])

    def over_levels(pair_out, other_out):
        other_in = lax.ppermute(other_out, "dur", others)
        return other_in, lax.ppermute(pair_out, "dur", pairs)

    *weights, rates = pl.pallas_call(
        weights_kernel,
        out_shape=(
            pltpu.VMEM((2 * states, states), BF16),
            pltpu.VMEM((4 * rows, states), BF16),
            pltpu.VMEM((8, LANES), F32),
        ),
        in_specs=[VMEM] * 2,
        out_specs=(VMEM,) * 3,
        scratch_shapes=[pltpu.VMEM((states, states), F32)],
        name="weights",
    )(*in_vmem(markov, tax))
    fixed = pl.pallas_call(
        functools.partial(fixed_kernel, scale),
        out_shape=pair,
        in_specs=[VMEM] * 3,
        out_specs=VMEM,
        name="fixed",
    )(*in_vmem(energy_share, mass_start, bwd_bracket))
    pair_out, other_out, kept = pl.pallas_call(
        open_kernel,
        out_shape=(pair, pair, slab),
        in_specs=[VMEM] * 6,
        out_specs=(VMEM,) * 3,
        scratch_shapes=push_scratch,
        name="open",
    )(value_next, mass_start, fwd_bracket, fwd_weight, dur_step, dur_weight)
    halo = over_levels(pair_out, other_out)
    mine = pl.pallas_call(
        merge_kernel,
        out_shape=pltpu.VMEM((4 * rows, assets), F32),
        in_specs=[VMEM] * 5,
        out_specs=VMEM,
        name="merge_with_fixed",
    )(*in_vmem(kept, value_next, *halo, fixed))
    every_first = [mine] + over_chips(mine)
    keep, send = pl.pallas_call(
        markov_kernel,
        out_shape=(pair, pair),
        in_specs=[VMEM] * 6,
        out_specs=(VMEM, VMEM),
        scratch_shapes=[pltpu.VMEM((states, assets), F32), pltpu.VMEM((2 * rows, assets), F32)],
        name="markov",
    )(*in_vmem(*every_first, *weights))
    pair_out, other_out, kept, value, second = pl.pallas_call(
        functools.partial(turn_kernel, scale),
        out_shape=(pair, pair, slab, slab, eight),
        in_specs=[VMEM] * 10,
        out_specs=(VMEM,) * 5,
        scratch_shapes=push_scratch,
        name="turn",
    )(
        *in_vmem(keep, over_cores(send), bwd_bracket, bwd_weight, energy_share, rates),
        *in_vmem(fwd_bracket, fwd_weight, dur_step, dur_weight),
    )
    halo = over_levels(pair_out, other_out)
    mine = pl.pallas_call(
        merge_kernel,
        out_shape=pltpu.VMEM((3 * rows + 8, assets), F32),
        in_specs=[VMEM] * 6,
        out_specs=VMEM,
        name="merge_with_demand",
    )(*in_vmem(kept, value, *halo, second, bwd_weight))
    every_second = [mine] + over_chips(mine)
    wide = pltpu.VMEM(((1 + chips) * rows, assets), F32)
    keep, send, second = pl.pallas_call(
        markov_wide_kernel,
        out_shape=(wide, wide, eight),
        in_specs=[VMEM] * 6,
        out_specs=(VMEM,) * 3,
        scratch_shapes=[
            pltpu.VMEM((states, assets), F32),
            pltpu.VMEM((states, assets), F32),
            pltpu.VMEM((chips, 8, assets), F32),
        ],
        name="markov_wide",
    )(*in_vmem(*every_second, *weights))
    value_start, mass_end, terms = pl.pallas_call(
        close_kernel,
        out_shape=(block, block, pltpu.VMEM((levels * cores, 1, LANES), F32)),
        in_specs=[VMEM] * 13,
        out_specs=(pl.BlockSpec(memory_space=pl.ANY),) * 2 + (VMEM,),
        scratch_shapes=[
            pltpu.VMEM((2, 1, rows, assets), F32),
            pltpu.VMEM((chips, 8, LANES), F32),
            pltpu.SemaphoreType.DMA((2,)),
        ],
        name="close",
    )(*in_vmem(keep, over_cores(send), *every_first, *every_second, energy_share, rates, second))
    every_term = lax.all_to_all(terms, ("dur", "core"), 0, 0)
    demand = pl.pallas_call(
        demand_kernel,
        out_shape=jax.ShapeDtypeStruct((2,), F32),
        in_specs=[VMEM],
        out_specs=VMEM,
        name="demand",
    )(*in_vmem(every_term))
    return (value_start, mass_end, demand)


def solution(mesh):
    levels, incs = mesh.devices.shape
    mesh = Mesh(mesh.devices.reshape(levels, incs // 2, 2), ("dur", "x", "core"))
    inc = ("x", "core")
    return jax.shard_map(
        per_device,
        mesh=mesh,
        in_specs=(
            P("dur", inc, None),
            P(),
            P("dur", inc, None),
            P(None, "dur", inc, None),
            P(None, "dur", inc, None),
            P(None, "dur", inc, None),
            P(None, "dur", inc, None),
            P(None, "dur", inc, None),
            P(None, "dur", inc, None),
            P("dur", inc, None),
            P(),
        ),
        out_specs=(P("dur", inc, None), P("dur", inc, None), P()),
        check_vma=False,
    )
```

```python
import functools

import jax
import jax.numpy as jnp
from jax import lax
from jax.experimental import pallas as pl
from jax.experimental.pallas import tpu as pltpu
from jax.sharding import Mesh, PartitionSpec as P

discount = 0.985
gross_rate = 1.01
adjust_share = 0.3

LANES = 128
SHIFTS = (0, 1, 3, 2)
F32 = jnp.float32
BF16 = jnp.bfloat16
VMEM = pl.BlockSpec(memory_space=pltpu.VMEM)


def in_vmem(*arrays):
    return tuple(pltpu.with_memory_space_constraint(x, pltpu.VMEM) for x in arrays)


def split_bf16(x):
    high = x.astype(BF16)
    return high, (x - high.astype(F32)).astype(BF16)


def bracket_read(mixed, bracket, weight):
    rows, assets = mixed.shape
    chunks = assets // LANES
    upper = pltpu.roll(mixed, assets - 1, 1)
    chunk_of = bracket >> (LANES.bit_length() - 1)
    lane_of = bracket & (LANES - 1)

    def chosen(values, chunk, first):
        if len(values) == 1:
            return values[0]
        half = len(values) // 2
        return jnp.where(
            chunk < first + half, chosen(values[:half], chunk, first), chosen(values[half:], chunk, first + half)
        )

    groups = []
    for top in range(0, rows, 8):
        part = slice(top, top + 8)
        pieces = []
        for out in range(chunks):
            span = slice(out * LANES, (out + 1) * LANES)
            lane, chunk, lam = lane_of[part, span], chunk_of[part, span], weight[part, span]
            low, high = (
                chosen(
                    [
                        jnp.take_along_axis(
                            table[part, k * LANES : (k + 1) * LANES], lane, axis=1, mode="promise_in_bounds"
                        )
                        for k in range(chunks)
                    ],
                    chunk,
                    0,
                )
                for table in (mixed, upper)
            )
            pieces.append((1.0 - lam) * low + lam * high)
        groups.append(jnp.concatenate(pieces, axis=1))
    return jnp.concatenate(groups, axis=0)


def push_assets(density, bracket, weight, parts_ref, sums_ref):
    rows, assets = density.shape
    width = LANES // 2
    chunks = assets // width
    chunk_of = bracket >> (width.bit_length() - 1)
    place_of = bracket & (width - 1)
    share = weight * density
    for k, value in enumerate((density - share, share)):
        high, low = split_bf16(value)
        parts_ref[2 * k] = high.astype(F32)
        parts_ref[2 * k + 1] = low.astype(F32)
    height = 4 * chunks
    chunk_iota = lax.broadcasted_iota(jnp.int32, (chunks, assets), 0)
    place_iota = lax.broadcasted_iota(jnp.int32, (width, assets), 0)
    for r in range(rows):
        row = slice(r, r + 1)
        here = chunk_iota == chunk_of[row, :]
        left = jnp.concatenate([jnp.where(here, parts_ref[k, row, :], 0.0) for k in range(4)], axis=0).astype(BF16)
        right = jnp.where(place_iota == place_of[row, :], 1.0, 0.0).astype(BF16)
        sums_ref[r * height : (r + 1) * height, :width] = lax.dot_general(
            left, right, (((1,), (1,)), ((), ())), preferred_element_type=F32
        )
    low_half = lax.broadcasted_iota(jnp.int32, (rows, LANES), 1) < width

    def gathered(k, h):
        high, low = (sums_ref[pl.ds((k + term) * chunks + h, rows, stride=height), :] for term in range(2))
        return high + low

    def assembled(k):
        return jnp.concatenate(
            [
                jnp.where(low_half, gathered(k, h), pltpu.roll(gathered(k, h + 1), width, 1))
                for h in range(0, chunks, 2)
            ],
            axis=1,
        )

    return assembled(0) + pltpu.roll(assembled(2), 1, 1)


def level_shares(moved, step, omega):
    level = lax.axis_index("dur")
    total = lax.axis_size("dur")
    lower = jnp.clip(level + step, 0, total - 2)
    down = lower - level == -1
    upper_part = moved * omega
    lower_part = moved - upper_part
    to_self = jnp.where(down, upper_part, lower_part)
    to_minus = jnp.where(down, lower_part, 0.0)
    to_plus = jnp.where(down, 0.0, upper_part)
    return to_self, to_plus, to_minus


def store_halo(pair_ref, other_ref, to_plus, to_minus, value):
    rows = value.shape[0]
    even = lax.axis_index("dur") % 2 == 0
    pair_ref[:rows, :] = jnp.where(even, to_plus, to_minus)
    other_ref[:rows, :] = jnp.where(even, to_minus, to_plus)
    pair_ref[rows:, :] = value
    other_ref[rows:, :] = value


def weights_kernel(markov_ref, tax_ref, back_ref, ahead_ref, rates_ref, flip_ref):
    taxes = tax_ref[...].reshape(1, 2)
    for quarter in range(2):
        tax = jnp.broadcast_to(taxes[:, quarter : quarter + 1], (1, LANES))
        rates_ref[quarter : quarter + 1, :] = tax
        rates_ref[2 + quarter : 3 + quarter, :] = 1.0 / (1.0 + tax)
    chip = lax.axis_index("x")
    states = markov_ref.shape[0]
    wide = ahead_ref.shape[0] // 2
    flip_ref[...] = markov_ref[...].T
    high, low = split_bf16(discount * markov_ref[...])
    back_ref[:states, :] = high
    back_ref[states:, :] = low
    high, low = split_bf16(flip_ref[pl.ds(pl.multiple_of(chip * wide, wide), wide), :])
    ahead_ref[:wide, :] = high
    ahead_ref[wide:, :] = low


def fixed_kernel(scale, energy_ref, mass_ref, bracket_ref, out_ref):
    rows = energy_ref.shape[1]
    out_ref[:rows, :] = scale * mass_ref[0] * energy_ref[0]
    out_ref[rows:, :] = bracket_ref[0, 0].astype(F32)


def open_kernel(
    mass_ref, bracket_ref, weight_ref, step_ref, omega_ref, value_ref, pair_ref, other_ref, self_ref, floats_ref, ints_ref,
    sems, parts_ref, sums_ref,
):
    copies = [
        pltpu.make_async_copy(source, target, sems.at[k])
        for k, (source, target) in enumerate(
            (
                (mass_ref.at[0], floats_ref.at[0]),
                (bracket_ref.at[0, 0], ints_ref.at[0]),
                (weight_ref.at[0, 0], floats_ref.at[1]),
                (step_ref.at[0, 0], ints_ref.at[1]),
                (omega_ref.at[0, 0], floats_ref.at[2]),
                (value_ref.at[0], floats_ref.at[3]),
            )
        )
    ]
    for copy in copies:
        copy.start()
    for copy in copies[:3]:
        copy.wait()
    moved = push_assets(floats_ref[0], ints_ref[0], floats_ref[1], parts_ref, sums_ref)
    for copy in copies[3:]:
        copy.wait()
    to_self, to_plus, to_minus = level_shares(moved, ints_ref[1], floats_ref[2])
    self_ref[...] = to_self
    store_halo(pair_ref, other_ref, to_plus, to_minus, floats_ref[3])


def merge_kernel(self_ref, value_ref, other_ref, pair_ref, *rest):
    *rider_refs, out_ref = rest
    rows = self_ref.shape[0]
    level = lax.axis_index("dur")
    value = value_ref[...].reshape(self_ref.shape)
    alone = (level == 0) | (level == lax.axis_size("dur") - 1)
    beside = pair_ref[rows:, :] + jnp.where(alone, value, other_ref[rows:, :])
    incoming = pair_ref[:rows, :] + jnp.where(alone, 0.0, other_ref[:rows, :])
    out_ref[:rows, :] = self_ref[...] + incoming
    out_ref[rows : 2 * rows, :] = (1.0 - adjust_share) * value + adjust_share * 0.5 * beside
    top = 2 * rows
    for ref in rider_refs:
        rider = ref[0, 0] if len(ref.shape) == 4 else ref[...]
        out_ref[top : top + rider.shape[0], :] = rider
        top += rider.shape[0]


def place_field(refs, part, rows, field_ref):
    chip, core = lax.axis_index("x"), lax.axis_index("core")
    field_ref[...] = jnp.zeros_like(field_ref)
    for shift, ref in zip(SHIFTS, refs):
        at = pl.ds(pl.multiple_of((chip ^ shift) * 2 * rows + core * rows, rows), rows)
        field_ref[at, :] = ref[part * rows : (part + 1) * rows, :]
    return split_bf16(field_ref[...])


def product(factor_high, factor_low, high, low):
    count = factor_high.shape[0]
    both = jnp.dot(jnp.concatenate([factor_high, factor_low], axis=0), high, preferred_element_type=F32)
    return both[:count] + (both[count:] + jnp.dot(factor_high, low, preferred_element_type=F32))


def markov_kernel(
    own_ref, one_ref, two_ref, three_ref, back_ref, ahead_ref, keep_ref, send_ref, field_ref, total_ref
):
    refs = (own_ref, one_ref, two_ref, three_ref)
    chip, core = lax.axis_index("x"), lax.axis_index("core")
    states = back_ref.shape[0] // 2
    wide = ahead_ref.shape[0] // 2
    rows = wide // 2
    mine = pl.ds(pl.multiple_of(core * rows, rows), rows)
    theirs = pl.ds(pl.multiple_of((1 - core) * rows, rows), rows)
    total_ref[:wide, :] = product(ahead_ref[:wide, :], ahead_ref[wide:, :], *place_field(refs, 0, rows, field_ref))
    keep_ref[:rows, :] = total_ref[mine, :]
    send_ref[:rows, :] = total_ref[theirs, :]
    at = pl.multiple_of(chip * wide, wide)
    total_ref[:wide, :] = product(
        back_ref[pl.ds(at, wide), :],
        back_ref[pl.ds(states + at, wide), :],
        *place_field(refs, 1, rows, field_ref),
    )
    keep_ref[rows:, :] = total_ref[mine, :]
    send_ref[rows:, :] = total_ref[theirs, :]


def markov_wide_kernel(
    own_ref, one_ref, two_ref, three_ref, back_ref, ahead_ref, keep_ref, send_ref, demand_ref, field_ref, total_ref,
    terms_ref,
):
    refs = (own_ref, one_ref, two_ref, three_ref)
    chip, core = lax.axis_index("x"), lax.axis_index("core")
    states = back_ref.shape[0] // 2
    wide = ahead_ref.shape[0] // 2
    rows = wide // 2
    mine = pl.ds(pl.multiple_of(core * rows, rows), rows)
    theirs = pl.ds(pl.multiple_of((1 - core) * rows, rows), rows)
    total_ref[:wide, :] = product(ahead_ref[:wide, :], ahead_ref[wide:, :], *place_field(refs, 0, rows, field_ref))
    keep_ref[:rows, :] = total_ref[mine, :]
    send_ref[:rows, :] = total_ref[theirs, :]
    total_ref[...] = product(back_ref[:states, :], back_ref[states:, :], *place_field(refs, 1, rows, field_ref))
    for k in range(len(refs)):
        part = slice((k + 1) * rows, (k + 2) * rows)
        keep_ref[part, :] = total_ref[pl.ds(pl.multiple_of(k * wide + core * rows, rows), rows), :]
        send_ref[part, :] = total_ref[pl.ds(pl.multiple_of(k * wide + (1 - core) * rows, rows), rows), :]
    for shift, ref in zip(SHIFTS, refs):
        terms_ref[chip ^ shift] = ref[2 * rows : 2 * rows + demand_ref.shape[0], :]
    demand_ref[...] = (terms_ref[0] + terms_ref[1]) + (terms_ref[2] + terms_ref[3])


def turn_kernel(
    scale, keep_ref, got_ref, bracket_ref, lam_ref, energy_ref, rates_ref, fwd_bracket_ref, fwd_weight_ref, step_ref,
    omega_ref, pair_ref, other_ref, self_ref, value_ref, demand_ref, parts_ref, sums_ref,
):
    rows = self_ref.shape[0]
    density = keep_ref[:rows, :] + got_ref[:rows, :]
    mixed = keep_ref[rows:, :] + got_ref[rows:, :]
    interp = bracket_read(mixed, bracket_ref[1, 0], lam_ref[1, 0])
    tax = rates_ref[1:2, :1]
    share = energy_ref[0]
    spent = density * (share * lax.rsqrt(interp))
    half = demand_ref.shape[0]
    demand_ref[...] = (scale * rates_ref[3:4, :1]) * sum(spent[k : k + half] for k in range(0, rows, half))
    value = gross_rate * interp * (1.0 + tax * share)
    moved = push_assets(density, fwd_bracket_ref[1, 0], fwd_weight_ref[1, 0], parts_ref, sums_ref)
    to_self, to_plus, to_minus = level_shares(moved, step_ref[1, 0], omega_ref[1, 0])
    self_ref[...] = to_self
    value_ref[...] = value
    store_halo(pair_ref, other_ref, to_plus, to_minus, value)


def folded(terms):
    return sum(
        terms[top : top + 8, left : left + LANES]
        for top in range(0, terms.shape[0], 8)
        for left in range(0, terms.shape[1], LANES)
    )


def close_kernel(keep_ref, got_ref, *rest):
    (*rider_refs, energy_ref, rates_ref, demand_ref, value_ref, mass_ref, terms_ref, out_ref, spent_ref, sems) = rest
    rows = energy_ref.shape[1]
    chip = lax.axis_index("x")
    tax, shrink = rates_ref[:1, :1], rates_ref[2:3, :1]
    out_ref[1, 0] = keep_ref[:rows, :] + got_ref[:rows, :]
    mass_copy = pltpu.make_async_copy(out_ref.at[1], mass_ref, sems.at[1])
    mass_copy.start()
    value_copy = pltpu.make_async_copy(out_ref.at[0], value_ref, sems.at[0])
    for shift, ref, later_ref in zip(SHIFTS, rider_refs[: len(SHIFTS)], rider_refs[len(SHIFTS) :]):
        part = pl.ds(pl.multiple_of(((chip ^ shift) + 1) * rows, rows), rows)
        bracket = ref[3 * rows : 4 * rows, :].astype(jnp.int32)
        interp = bracket_read(keep_ref[part, :] + got_ref[part, :], bracket, later_ref[later_ref.shape[0] - rows :, :])
        spent = ref[2 * rows : 3 * rows, :] * lax.rsqrt(interp)
        spent_ref[chip ^ shift] = folded(spent)
        if shift == 0:
            out_ref[0, 0] = gross_rate * interp * (1.0 + tax * energy_ref[0])
            value_copy.start()
    first = jnp.sum((spent_ref[0] + spent_ref[1]) + (spent_ref[2] + spent_ref[3]), axis=(0, 1), keepdims=True)
    first = first * shrink
    second = jnp.sum(folded(demand_ref[...]), axis=(0, 1), keepdims=True)
    lane = lax.broadcasted_iota(jnp.int32, (1, LANES), 1)
    terms_ref[...] = jnp.broadcast_to(jnp.where(lane == 0, first, second)[None], terms_ref.shape)
    mass_copy.wait()
    value_copy.wait()


def demand_kernel(terms_ref, out_ref):
    out_ref[...] = jnp.sum(terms_ref[...], axis=0)[0, : out_ref.shape[0]]


def per_device(
    value_next,
    markov,
    energy_share,
    bwd_bracket,
    bwd_weight,
    fwd_bracket,
    fwd_weight,
    dur_step,
    dur_weight,
    mass_start,
    tax,
):
    _, rows, assets = value_next.shape
    states = markov.shape[0]
    levels, chips, cores = (lax.axis_size(axis) for axis in ("dur", "x", "core"))
    scale = 1.0 / (levels * states * assets)
    chunks = assets // (LANES // 2)
    slab = pltpu.VMEM((rows, assets), F32)
    pair = pltpu.VMEM((2 * rows, assets), F32)
    block = jax.ShapeDtypeStruct((1, rows, assets), F32)
    eight = pltpu.VMEM((8, assets), F32)
    push_scratch = [pltpu.VMEM((4, rows, assets), F32), pltpu.VMEM((rows * 4 * chunks, LANES), F32)]
    pairs = [(i, i ^ 1) for i in range(levels)]
    others = [(i, ((i + 1) ^ 1) - 1) for i in range(1, levels - 1)]

    def over_chips(array):
        return [lax.ppermute(array, "x", [(i, i ^ k) for i in range(chips)]) for k in SHIFTS[1:]]

    def over_cores(array):
        return lax.ppermute(array, "core", [(i, i ^ 1) for i in range(cores)])

    def over_levels(pair_out, other_out):
        other_in = lax.ppermute(other_out, "dur", others)
        return other_in, lax.ppermute(pair_out, "dur", pairs)

    *weights, rates = pl.pallas_call(
        weights_kernel,
        out_shape=(
            pltpu.VMEM((2 * states, states), BF16),
            pltpu.VMEM((4 * rows, states), BF16),
            pltpu.VMEM((8, LANES), F32),
        ),
        in_specs=[VMEM] * 2,
        out_specs=(VMEM,) * 3,
        scratch_shapes=[pltpu.VMEM((states, states), F32)],
        name="weights",
    )(*in_vmem(markov, tax))
    fixed = pl.pallas_call(
        functools.partial(fixed_kernel, scale),
        out_shape=pair,
        in_specs=[VMEM] * 3,
        out_specs=VMEM,
        name="fixed",
    )(*in_vmem(energy_share, mass_start, bwd_bracket))
    pair_out, other_out, kept = pl.pallas_call(
        open_kernel,
        out_shape=(pair, pair, slab),
        in_specs=[pl.BlockSpec(memory_space=pl.ANY)] * 6,
        out_specs=(VMEM,) * 3,
        scratch_shapes=[
            pltpu.VMEM((4, rows, assets), F32),
            pltpu.VMEM((2, rows, assets), jnp.int32),
            pltpu.SemaphoreType.DMA((6,)),
            *push_scratch,
        ],
        name="open",
    )(mass_start, fwd_bracket, fwd_weight, dur_step, dur_weight, value_next)
    halo = over_levels(pair_out, other_out)
    mine = pl.pallas_call(
        merge_kernel,
        out_shape=pltpu.VMEM((4 * rows, assets), F32),
        in_specs=[VMEM] * 5,
        out_specs=VMEM,
        name="merge_with_fixed",
    )(*in_vmem(kept, value_next, *halo, fixed))
    every_first = [mine] + over_chips(mine)
    keep, send = pl.pallas_call(
        markov_kernel,
        out_shape=(pair, pair),
        in_specs=[VMEM] * 6,
        out_specs=(VMEM, VMEM),
        scratch_shapes=[pltpu.VMEM((states, assets), F32), pltpu.VMEM((2 * rows, assets), F32)],
        name="markov",
    )(*in_vmem(*every_first, *weights))
    pair_out, other_out, kept, value, second = pl.pallas_call(
        functools.partial(turn_kernel, scale),
        out_shape=(pair, pair, slab, slab, eight),
        in_specs=[VMEM] * 10,
        out_specs=(VMEM,) * 5,
        scratch_shapes=push_scratch,
        name="turn",
    )(
        *in_vmem(keep, over_cores(send), bwd_bracket, bwd_weight, energy_share, rates),
        *in_vmem(fwd_bracket, fwd_weight, dur_step, dur_weight),
    )
    halo = over_levels(pair_out, other_out)
    mine = pl.pallas_call(
        merge_kernel,
        out_shape=pltpu.VMEM((3 * rows + 8, assets), F32),
        in_specs=[VMEM] * 6,
        out_specs=VMEM,
        name="merge_with_demand",
    )(*in_vmem(kept, value, *halo, second, bwd_weight))
    every_second = [mine] + over_chips(mine)
    wide = pltpu.VMEM(((1 + chips) * rows, assets), F32)
    keep, send, second = pl.pallas_call(
        markov_wide_kernel,
        out_shape=(wide, wide, eight),
        in_specs=[VMEM] * 6,
        out_specs=(VMEM,) * 3,
        scratch_shapes=[
            pltpu.VMEM((states, assets), F32),
            pltpu.VMEM((states, assets), F32),
            pltpu.VMEM((chips, 8, assets), F32),
        ],
        name="markov_wide",
    )(*in_vmem(*every_second, *weights))
    value_start, mass_end, terms = pl.pallas_call(
        close_kernel,
        out_shape=(block, block, pltpu.VMEM((levels * cores, 1, LANES), F32)),
        in_specs=[VMEM] * 13,
        out_specs=(pl.BlockSpec(memory_space=pl.ANY),) * 2 + (VMEM,),
        scratch_shapes=[
            pltpu.VMEM((2, 1, rows, assets), F32),
            pltpu.VMEM((chips, 8, LANES), F32),
            pltpu.SemaphoreType.DMA((2,)),
        ],
        name="close",
    )(*in_vmem(keep, over_cores(send), *every_first, *every_second, energy_share, rates, second))
    every_term = lax.all_to_all(terms, ("dur", "core"), 0, 0)
    demand = pl.pallas_call(
        demand_kernel,
        out_shape=jax.ShapeDtypeStruct((2,), F32),
        in_specs=[VMEM],
        out_specs=VMEM,
        name="demand",
    )(*in_vmem(every_term))
    return (value_start, mass_end, demand)


def solution(mesh):
    levels, incs = mesh.devices.shape
    mesh = Mesh(mesh.devices.reshape(levels, incs // 2, 2), ("dur", "x", "core"))
    inc = ("x", "core")
    return jax.shard_map(
        per_device,
        mesh=mesh,
        in_specs=(
            P("dur", inc, None),
            P(),
            P("dur", inc, None),
            P(None, "dur", inc, None),
            P(None, "dur", inc, None),
            P(None, "dur", inc, None),
            P(None, "dur", inc, None),
            P(None, "dur", inc, None),
            P(None, "dur", inc, None),
            P("dur", inc, None),
            P(),
        ),
        out_specs=(P("dur", inc, None), P("dur", inc, None), P()),
        check_vma=False,
    )
```

```python
import functools

import jax
import jax.numpy as jnp
from jax import lax
from jax.experimental import pallas as pl
from jax.experimental.pallas import tpu as pltpu
from jax.sharding import Mesh, PartitionSpec as P

discount = 0.985
gross_rate = 1.01
adjust_share = 0.3

LANES = 128
SHIFTS = (0, 1, 3, 2)
F32 = jnp.float32
BF16 = jnp.bfloat16
VMEM = pl.BlockSpec(memory_space=pltpu.VMEM)


def in_vmem(*arrays):
    return tuple(pltpu.with_memory_space_constraint(x, pltpu.VMEM) for x in arrays)


def split_bf16(x):
    high = x.astype(BF16)
    return high, (x - high.astype(F32)).astype(BF16)


def bracket_read(mixed, bracket, weight):
    rows, assets = mixed.shape
    chunks = assets // LANES
    upper = pltpu.roll(mixed, assets - 1, 1)
    chunk_of = bracket >> (LANES.bit_length() - 1)
    lane_of = bracket & (LANES - 1)

    def chosen(values, chunk, first):
        if len(values) == 1:
            return values[0]
        half = len(values) // 2
        return jnp.where(
            chunk < first + half, chosen(values[:half], chunk, first), chosen(values[half:], chunk, first + half)
        )

    groups = []
    for top in range(0, rows, 8):
        part = slice(top, top + 8)
        pieces = []
        for out in range(chunks):
            span = slice(out * LANES, (out + 1) * LANES)
            lane, chunk, lam = lane_of[part, span], chunk_of[part, span], weight[part, span]
            low, high = (
                chosen(
                    [
                        jnp.take_along_axis(
                            table[part, k * LANES : (k + 1) * LANES], lane, axis=1, mode="promise_in_bounds"
                        )
                        for k in range(chunks)
                    ],
                    chunk,
                    0,
                )
                for table in (mixed, upper)
            )
            pieces.append((1.0 - lam) * low + lam * high)
        groups.append(jnp.concatenate(pieces, axis=1))
    return jnp.concatenate(groups, axis=0)


def push_assets(density, bracket, weight, parts_ref, sums_ref):
    rows, assets = density.shape
    width = LANES // 2
    chunks = assets // width
    chunk_of = bracket >> (width.bit_length() - 1)
    place_of = bracket & (width - 1)
    share = weight * density
    for k, value in enumerate((density - share, share)):
        high, low = split_bf16(value)
        parts_ref[2 * k] = high.astype(F32)
        parts_ref[2 * k + 1] = low.astype(F32)
    height = 4 * chunks
    chunk_iota = lax.broadcasted_iota(jnp.int32, (chunks, assets), 0)
    place_iota = lax.broadcasted_iota(jnp.int32, (width, assets), 0)
    for r in range(rows):
        row = slice(r, r + 1)
        here = chunk_iota == chunk_of[row, :]
        left = jnp.concatenate([jnp.where(here, parts_ref[k, row, :], 0.0) for k in range(4)], axis=0).astype(BF16)
        right = jnp.where(place_iota == place_of[row, :], 1.0, 0.0).astype(BF16)
        sums_ref[r * height : (r + 1) * height, :width] = lax.dot_general(
            left, right, (((1,), (1,)), ((), ())), preferred_element_type=F32
        )
    low_half = lax.broadcasted_iota(jnp.int32, (rows, LANES), 1) < width

    def gathered(k, h):
        high, low = (sums_ref[pl.ds((k + term) * chunks + h, rows, stride=height), :] for term in range(2))
        return high + low

    def assembled(k):
        return jnp.concatenate(
            [
                jnp.where(low_half, gathered(k, h), pltpu.roll(gathered(k, h + 1), width, 1))
                for h in range(0, chunks, 2)
            ],
            axis=1,
        )

    return assembled(0) + pltpu.roll(assembled(2), 1, 1)


def level_shares(moved, step, omega):
    level = lax.axis_index("dur")
    total = lax.axis_size("dur")
    lower = jnp.clip(level + step, 0, total - 2)
    down = lower - level == -1
    upper_part = moved * omega
    lower_part = moved - upper_part
    to_self = jnp.where(down, upper_part, lower_part)
    to_minus = jnp.where(down, lower_part, 0.0)
    to_plus = jnp.where(down, 0.0, upper_part)
    return to_self, to_plus, to_minus


def store_halo(pair_ref, other_ref, to_plus, to_minus, value):
    rows = value.shape[0]
    even = lax.axis_index("dur") % 2 == 0
    pair_ref[:rows, :] = jnp.where(even, to_plus, to_minus)
    other_ref[:rows, :] = jnp.where(even, to_minus, to_plus)
    pair_ref[rows:, :] = value
    other_ref[rows:, :] = value


def weights_kernel(markov_ref, tax_ref, back_ref, ahead_ref, rates_ref, flip_ref):
    taxes = tax_ref[...].reshape(1, 2)
    for quarter in range(2):
        tax = jnp.broadcast_to(taxes[:, quarter : quarter + 1], (1, LANES))
        rates_ref[quarter : quarter + 1, :] = tax
        rates_ref[2 + quarter : 3 + quarter, :] = 1.0 / (1.0 + tax)
    chip = lax.axis_index("x")
    states = markov_ref.shape[0]
    wide = ahead_ref.shape[0] // 2
    flip_ref[...] = markov_ref[...].T
    high, low = split_bf16(discount * markov_ref[...])
    back_ref[:states, :] = high
    back_ref[states:, :] = low
    high, low = split_bf16(flip_ref[pl.ds(pl.multiple_of(chip * wide, wide), wide), :])
    ahead_ref[:wide, :] = high
    ahead_ref[wide:, :] = low


def fixed_kernel(scale, energy_ref, mass_ref, bracket_ref, out_ref):
    rows = energy_ref.shape[1]
    out_ref[:rows, :] = scale * mass_ref[0] * energy_ref[0]
    out_ref[rows:, :] = bracket_ref[0, 0].astype(F32)


def open_kernel(
    mass_ref, bracket_ref, weight_ref, step_ref, omega_ref, value_ref, pair_ref, other_ref, self_ref, floats_ref, ints_ref,
    sems, parts_ref, sums_ref,
):
    copies = [
        pltpu.make_async_copy(source, target, sems.at[k])
        for k, (source, target) in enumerate(
            (
                (mass_ref.at[0], floats_ref.at[0]),
                (bracket_ref.at[0, 0], ints_ref.at[0]),
                (weight_ref.at[0, 0], floats_ref.at[1]),
                (step_ref.at[0, 0], ints_ref.at[1]),
                (omega_ref.at[0, 0], floats_ref.at[2]),
                (value_ref.at[0], floats_ref.at[3]),
            )
        )
    ]
    for copy in copies:
        copy.start()
    for copy in copies[:3]:
        copy.wait()
    moved = push_assets(floats_ref[0], ints_ref[0], floats_ref[1], parts_ref, sums_ref)
    for copy in copies[3:]:
        copy.wait()
    to_self, to_plus, to_minus = level_shares(moved, ints_ref[1], floats_ref[2])
    self_ref[...] = to_self
    store_halo(pair_ref, other_ref, to_plus, to_minus, floats_ref[3])


def merge_kernel(self_ref, value_ref, other_ref, pair_ref, *rest):
    *rider_refs, out_ref = rest
    rows = self_ref.shape[0]
    level = lax.axis_index("dur")
    value = value_ref[...].reshape(self_ref.shape)
    alone = (level == 0) | (level == lax.axis_size("dur") - 1)
    beside = pair_ref[rows:, :] + jnp.where(alone, value, other_ref[rows:, :])
    incoming = pair_ref[:rows, :] + jnp.where(alone, 0.0, other_ref[:rows, :])
    out_ref[:rows, :] = self_ref[...] + incoming
    out_ref[rows : 2 * rows, :] = (1.0 - adjust_share) * value + adjust_share * 0.5 * beside
    top = 2 * rows
    for ref in rider_refs:
        rider = ref[0, 0] if len(ref.shape) == 4 else ref[...]
        out_ref[top : top + rider.shape[0], :] = rider
        top += rider.shape[0]


def place_field(refs, part, rows, field_ref):
    chip, core = lax.axis_index("x"), lax.axis_index("core")
    if part == 0:
        field_ref[...] = jnp.zeros_like(field_ref)
    for shift, ref in zip(SHIFTS, refs):
        at = pl.ds(pl.multiple_of((chip ^ shift) * 2 * rows + core * rows, rows), rows)
        field_ref[at, :] = ref[part * rows : (part + 1) * rows, :]
    return split_bf16(field_ref[...])


def product(factor_high, factor_low, high, low):
    count = factor_high.shape[0]
    both = jnp.dot(jnp.concatenate([factor_high, factor_low], axis=0), high, preferred_element_type=F32)
    return both[:count] + (both[count:] + jnp.dot(factor_high, low, preferred_element_type=F32))


def markov_kernel(
    own_ref, one_ref, two_ref, three_ref, back_ref, ahead_ref, keep_ref, send_ref, field_ref, total_ref
):
    refs = (own_ref, one_ref, two_ref, three_ref)
    chip, core = lax.axis_index("x"), lax.axis_index("core")
    states = back_ref.shape[0] // 2
    wide = ahead_ref.shape[0] // 2
    rows = wide // 2
    mine = pl.ds(pl.multiple_of(core * rows, rows), rows)
    theirs = pl.ds(pl.multiple_of((1 - core) * rows, rows), rows)
    total_ref[:wide, :] = product(ahead_ref[:wide, :], ahead_ref[wide:, :], *place_field(refs, 0, rows, field_ref))
    keep_ref[:rows, :] = total_ref[mine, :]
    send_ref[:rows, :] = total_ref[theirs, :]
    at = pl.multiple_of(chip * wide, wide)
    total_ref[:wide, :] = product(
        back_ref[pl.ds(at, wide), :],
        back_ref[pl.ds(states + at, wide), :],
        *place_field(refs, 1, rows, field_ref),
    )
    keep_ref[rows:, :] = total_ref[mine, :]
    send_ref[rows:, :] = total_ref[theirs, :]


def markov_wide_kernel(
    own_ref, one_ref, two_ref, three_ref, back_ref, ahead_ref, keep_ref, send_ref, demand_ref, field_ref, total_ref,
    terms_ref,
):
    refs = (own_ref, one_ref, two_ref, three_ref)
    chip, core = lax.axis_index("x"), lax.axis_index("core")
    states = back_ref.shape[0] // 2
    wide = ahead_ref.shape[0] // 2
    rows = wide // 2
    mine = pl.ds(pl.multiple_of(core * rows, rows), rows)
    theirs = pl.ds(pl.multiple_of((1 - core) * rows, rows), rows)
    total_ref[:wide, :] = product(ahead_ref[:wide, :], ahead_ref[wide:, :], *place_field(refs, 0, rows, field_ref))
    keep_ref[:rows, :] = total_ref[mine, :]
    send_ref[:rows, :] = total_ref[theirs, :]
    total_ref[...] = product(back_ref[:states, :], back_ref[states:, :], *place_field(refs, 1, rows, field_ref))
    for k in range(len(refs)):
        part = slice((k + 1) * rows, (k + 2) * rows)
        keep_ref[part, :] = total_ref[pl.ds(pl.multiple_of(k * wide + core * rows, rows), rows), :]
        send_ref[part, :] = total_ref[pl.ds(pl.multiple_of(k * wide + (1 - core) * rows, rows), rows), :]
    for shift, ref in zip(SHIFTS, refs):
        terms_ref[chip ^ shift] = ref[2 * rows : 2 * rows + demand_ref.shape[0], :]
    demand_ref[...] = (terms_ref[0] + terms_ref[1]) + (terms_ref[2] + terms_ref[3])


def turn_kernel(
    scale, keep_ref, got_ref, bracket_ref, lam_ref, energy_ref, rates_ref, fwd_bracket_ref, fwd_weight_ref, step_ref,
    omega_ref, pair_ref, other_ref, self_ref, value_ref, demand_ref, parts_ref, sums_ref,
):
    rows = self_ref.shape[0]
    density = keep_ref[:rows, :] + got_ref[:rows, :]
    mixed = keep_ref[rows:, :] + got_ref[rows:, :]
    interp = bracket_read(mixed, bracket_ref[1, 0], lam_ref[1, 0])
    tax = rates_ref[1:2, :1]
    share = energy_ref[0]
    spent = density * (share * lax.rsqrt(interp))
    half = demand_ref.shape[0]
    demand_ref[...] = (scale * rates_ref[3:4, :1]) * sum(spent[k : k + half] for k in range(0, rows, half))
    value = gross_rate * interp * (1.0 + tax * share)
    moved = push_assets(density, fwd_bracket_ref[1, 0], fwd_weight_ref[1, 0], parts_ref, sums_ref)
    to_self, to_plus, to_minus = level_shares(moved, step_ref[1, 0], omega_ref[1, 0])
    self_ref[...] = to_self
    value_ref[...] = value
    store_halo(pair_ref, other_ref, to_plus, to_minus, value)


def folded(terms):
    return sum(
        terms[top : top + 8, left : left + LANES]
        for top in range(0, terms.shape[0], 8)
        for left in range(0, terms.shape[1], LANES)
    )


def close_kernel(keep_ref, got_ref, *rest):
    (*rider_refs, energy_ref, rates_ref, demand_ref, value_ref, mass_ref, terms_ref, out_ref, spent_ref, sems) = rest
    rows = energy_ref.shape[1]
    chip = lax.axis_index("x")
    tax, shrink = rates_ref[:1, :1], rates_ref[2:3, :1]
    out_ref[1, 0] = keep_ref[:rows, :] + got_ref[:rows, :]
    mass_copy = pltpu.make_async_copy(out_ref.at[1], mass_ref, sems.at[1])
    mass_copy.start()
    value_copy = pltpu.make_async_copy(out_ref.at[0], value_ref, sems.at[0])
    for shift, ref, later_ref in zip(SHIFTS, rider_refs[: len(SHIFTS)], rider_refs[len(SHIFTS) :]):
        part = pl.ds(pl.multiple_of(((chip ^ shift) + 1) * rows, rows), rows)
        bracket = ref[3 * rows : 4 * rows, :].astype(jnp.int32)
        interp = bracket_read(keep_ref[part, :] + got_ref[part, :], bracket, later_ref[later_ref.shape[0] - rows :, :])
        spent = ref[2 * rows : 3 * rows, :] * lax.rsqrt(interp)
        spent_ref[chip ^ shift] = folded(spent)
        if shift == 0:
            out_ref[0, 0] = gross_rate * interp * (1.0 + tax * energy_ref[0])
            value_copy.start()
    first = jnp.sum((spent_ref[0] + spent_ref[1]) + (spent_ref[2] + spent_ref[3]), axis=(0, 1), keepdims=True)
    first = first * shrink
    second = jnp.sum(folded(demand_ref[...]), axis=(0, 1), keepdims=True)
    lane = lax.broadcasted_iota(jnp.int32, (1, LANES), 1)
    terms_ref[...] = jnp.broadcast_to(jnp.where(lane == 0, first, second)[None], terms_ref.shape)
    mass_copy.wait()
    value_copy.wait()


def demand_kernel(terms_ref, out_ref):
    out_ref[...] = jnp.sum(terms_ref[...], axis=0)[0, : out_ref.shape[0]]


def per_device(
    value_next,
    markov,
    energy_share,
    bwd_bracket,
    bwd_weight,
    fwd_bracket,
    fwd_weight,
    dur_step,
    dur_weight,
    mass_start,
    tax,
):
    _, rows, assets = value_next.shape
    states = markov.shape[0]
    levels, chips, cores = (lax.axis_size(axis) for axis in ("dur", "x", "core"))
    scale = 1.0 / (levels * states * assets)
    chunks = assets // (LANES // 2)
    slab = pltpu.VMEM((rows, assets), F32)
    pair = pltpu.VMEM((2 * rows, assets), F32)
    block = jax.ShapeDtypeStruct((1, rows, assets), F32)
    eight = pltpu.VMEM((8, assets), F32)
    push_scratch = [pltpu.VMEM((4, rows, assets), F32), pltpu.VMEM((rows * 4 * chunks, LANES), F32)]
    pairs = [(i, i ^ 1) for i in range(levels)]
    others = [(i, ((i + 1) ^ 1) - 1) for i in range(1, levels - 1)]

    def over_chips(array):
        return [lax.ppermute(array, "x", [(i, i ^ k) for i in range(chips)]) for k in SHIFTS[1:]]

    def over_cores(array):
        return lax.ppermute(array, "core", [(i, i ^ 1) for i in range(cores)])

    def over_levels(pair_out, other_out):
        other_in = lax.ppermute(other_out, "dur", others)
        return other_in, lax.ppermute(pair_out, "dur", pairs)

    *weights, rates = pl.pallas_call(
        weights_kernel,
        out_shape=(
            pltpu.VMEM((2 * states, states), BF16),
            pltpu.VMEM((4 * rows, states), BF16),
            pltpu.VMEM((8, LANES), F32),
        ),
        in_specs=[VMEM] * 2,
        out_specs=(VMEM,) * 3,
        scratch_shapes=[pltpu.VMEM((states, states), F32)],
        name="weights",
    )(*in_vmem(markov, tax))
    fixed = pl.pallas_call(
        functools.partial(fixed_kernel, scale),
        out_shape=pair,
        in_specs=[VMEM] * 3,
        out_specs=VMEM,
        name="fixed",
    )(*in_vmem(energy_share, mass_start, bwd_bracket))
    pair_out, other_out, kept = pl.pallas_call(
        open_kernel,
        out_shape=(pair, pair, slab),
        in_specs=[pl.BlockSpec(memory_space=pl.ANY)] * 6,
        out_specs=(VMEM,) * 3,
        scratch_shapes=[
            pltpu.VMEM((4, rows, assets), F32),
            pltpu.VMEM((2, rows, assets), jnp.int32),
            pltpu.SemaphoreType.DMA((6,)),
            *push_scratch,
        ],
        name="open",
    )(mass_start, fwd_bracket, fwd_weight, dur_step, dur_weight, value_next)
    halo = over_levels(pair_out, other_out)
    mine = pl.pallas_call(
        merge_kernel,
        out_shape=pltpu.VMEM((4 * rows, assets), F32),
        in_specs=[VMEM] * 5,
        out_specs=VMEM,
        name="merge_with_fixed",
    )(*in_vmem(kept, value_next, *halo, fixed))
    every_first = [mine] + over_chips(mine)
    keep, send = pl.pallas_call(
        markov_kernel,
        out_shape=(pair, pair),
        in_specs=[VMEM] * 6,
        out_specs=(VMEM, VMEM),
        scratch_shapes=[pltpu.VMEM((states, assets), F32), pltpu.VMEM((2 * rows, assets), F32)],
        name="markov",
    )(*in_vmem(*every_first, *weights))
    pair_out, other_out, kept, value, second = pl.pallas_call(
        functools.partial(turn_kernel, scale),
        out_shape=(pair, pair, slab, slab, eight),
        in_specs=[VMEM] * 10,
        out_specs=(VMEM,) * 5,
        scratch_shapes=push_scratch,
        name="turn",
    )(
        *in_vmem(keep, over_cores(send), bwd_bracket, bwd_weight, energy_share, rates),
        *in_vmem(fwd_bracket, fwd_weight, dur_step, dur_weight),
    )
    halo = over_levels(pair_out, other_out)
    mine = pl.pallas_call(
        merge_kernel,
        out_shape=pltpu.VMEM((3 * rows + 8, assets), F32),
        in_specs=[VMEM] * 6,
        out_specs=VMEM,
        name="merge_with_demand",
    )(*in_vmem(kept, value, *halo, second, bwd_weight))
    every_second = [mine] + over_chips(mine)
    wide = pltpu.VMEM(((1 + chips) * rows, assets), F32)
    keep, send, second = pl.pallas_call(
        markov_wide_kernel,
        out_shape=(wide, wide, eight),
        in_specs=[VMEM] * 6,
        out_specs=(VMEM,) * 3,
        scratch_shapes=[
            pltpu.VMEM((states, assets), F32),
            pltpu.VMEM((states, assets), F32),
            pltpu.VMEM((chips, 8, assets), F32),
        ],
        name="markov_wide",
    )(*in_vmem(*every_second, *weights))
    value_start, mass_end, terms = pl.pallas_call(
        close_kernel,
        out_shape=(block, block, pltpu.VMEM((levels * cores, 1, LANES), F32)),
        in_specs=[VMEM] * 13,
        out_specs=(pl.BlockSpec(memory_space=pl.ANY),) * 2 + (VMEM,),
        scratch_shapes=[
            pltpu.VMEM((2, 1, rows, assets), F32),
            pltpu.VMEM((chips, 8, LANES), F32),
            pltpu.SemaphoreType.DMA((2,)),
        ],
        name="close",
    )(*in_vmem(keep, over_cores(send), *every_first, *every_second, energy_share, rates, second))
    every_term = lax.all_to_all(terms, ("dur", "core"), 0, 0)
    demand = pl.pallas_call(
        demand_kernel,
        out_shape=jax.ShapeDtypeStruct((2,), F32),
        in_specs=[VMEM],
        out_specs=VMEM,
        name="demand",
    )(*in_vmem(every_term))
    return (value_start, mass_end, demand)


def solution(mesh):
    levels, incs = mesh.devices.shape
    mesh = Mesh(mesh.devices.reshape(levels, incs // 2, 2), ("dur", "x", "core"))
    inc = ("x", "core")
    return jax.shard_map(
        per_device,
        mesh=mesh,
        in_specs=(
            P("dur", inc, None),
            P(),
            P("dur", inc, None),
            P(None, "dur", inc, None),
            P(None, "dur", inc, None),
            P(None, "dur", inc, None),
            P(None, "dur", inc, None),
            P(None, "dur", inc, None),
            P(None, "dur", inc, None),
            P("dur", inc, None),
            P(),
        ),
        out_specs=(P("dur", inc, None), P("dur", inc, None), P()),
        check_vma=False,
    )
```
